32 devices in a mesh: section: 4 (over y, x), fsdp: 8 (over z, core).
Axes of the slice: x: 2, y: 2, z: 4, core: 2. Of those that a mesh axis runs over, the one named last changes fastest.
Arguments:
- inputs: bfloat16 [4, 8, 256, 4096], P('section', None, 'fsdp'), may hold values from -6 to 6
- upstream: bfloat16 [8, 256, 4096], P(None, 'fsdp'), may hold values from -6 to 6
- weights: bfloat16 [4, 4096, 512], P('section', 'fsdp')
- gain: bfloat16 [4, 4096], P('section', 'fsdp'), may hold values from 0.5 to 1.5
Outputs:
- weight_grad: float32 [4, 4096, 512], P('section', 'fsdp')
- gain_grad: float32 [4, 4096], P('section')
The draws below stay inside these ranges and needn't reach their ends.
All inputs are finite; a program needn't handle non-finite values.
Results may differ from the reference program's by a relative error of at most 0.035.
Values may be sent and summed in bfloat16 or wider, within the bound.
A program may use at most 128 MiB of HBM per device.

```python
import jax
import jax.numpy as jnp
from jax import lax

D = 4096
HD = 128
TMB = 32
MB = 8
SECTIONS = 4
TOKENS = 256
N_FSDP = 8


def draw_weights(key, part):
    layout = (SECTIONS, D, 4 * HD)
    return (jax.random.normal(key, layout, jnp.float32) * D ** (-0.5)).astype(jnp.bfloat16)


def shard_levels(own_key, extent, split, least, largest):
    def one(axis_at, blocks):
        steps = jax.random.uniform(jax.random.fold_in(jax.random.fold_in(own_key, 6), axis_at), (blocks,), jnp.float32, least / len(split), largest / len(split))
        return jnp.repeat(jnp.exp(steps), extent[axis_at] // blocks).reshape((-1,) + (1,) * (len(extent) - axis_at - 1))

    loudness = one(*split[0])
    for cut in split[1:]:
        loudness = loudness * one(*cut)
    return loudness


def centred(own_key, shape, scale, bound, split=(), kind=jnp.bfloat16):
    factor_of = shard_levels(own_key, shape, split, -0.22, 0.18) if split else 1.0
    values = jax.random.normal(own_key, shape, jnp.float32) * scale * factor_of
    return jnp.minimum(jnp.maximum(values, -bound), bound).astype(kind)


def setup_inputs(seed: int = 0) -> dict:
    key_of = jax.random.split(jax.random.key(seed), 5)
    inputs = centred(key_of[0], (SECTIONS, MB, TOKENS, D), 1.0, 6.0, ((0, 4), (2, 8)))
    upstream = centred(key_of[1], (MB, TOKENS, D), 1.0, 6.0, ((1, 8),))
    weights = draw_weights(jax.random.fold_in(key_of[4], 71), 0)
    gain = jnp.clip(0.5 + 1.0 * jax.random.uniform(key_of[3], (SECTIONS, D), jnp.float32) ** shard_levels(key_of[3], (SECTIONS, D), ((0, 4), (1, 8)), -0.2, 0.2), 0.5, 1.5).astype(jnp.bfloat16)
    return {"inputs": inputs, "upstream": upstream, "weights": weights, "gain": gain}


def rope_tables(length, head):
    half_head = head // 2
    position = jnp.arange(length, dtype=jnp.float32)
    freq = jnp.power(500000.0, -2.0 * jnp.arange(half_head, dtype=jnp.float32) / head)
    angle = position[:, None] * freq[None, :]
    return (jnp.cos(angle), jnp.sin(angle))

def rotate(value_rows, cosine, sine_table):
    half_head = value_rows.shape[-1] // 2
    first = value_rows[..., :half_head]
    second = value_rows[..., half_head:]
    return jnp.concatenate([first * cosine - second * sine_table, second * cosine + first * sine_table], axis=-1)

def unrotate(value_rows, cosine, sine_table):
    half_head = value_rows.shape[-1] // 2
    first = value_rows[..., :half_head]
    second = value_rows[..., half_head:]
    return jnp.concatenate([first * cosine + second * sine_table, second * cosine - first * sine_table], axis=-1)

def section_pass(inputs_m, weight, gain_row, grad_in):
    seqs, length, width = inputs_m.shape
    head = weight.shape[1] // 4
    cosine, sine_table = rope_tables(length, head)
    xfloat = inputs_m.astype(jnp.float32)
    inv_rms = lax.rsqrt(lax.optimization_barrier(jnp.mean(xfloat * xfloat, axis=-1, keepdims=True)) + 1e-05)
    normed = xfloat * inv_rms
    wide_gain = gain_row.astype(jnp.float32)
    hidden = (normed * wide_gain).astype(jnp.bfloat16)
    proj = jnp.dot(hidden.reshape(-1, width), weight[:, :3 * head], preferred_element_type=jnp.float32)
    proj = proj.reshape(seqs, length, 3 * head)
    query_rows = rotate(proj[..., :head], cosine, sine_table).astype(jnp.bfloat16)
    key_rows = rotate(proj[..., head:2 * head], cosine, sine_table).astype(jnp.bfloat16)
    value_rows = proj[..., 2 * head:].astype(jnp.bfloat16)
    score_scale = head ** (-0.5)
    score_matrix = jnp.einsum('onr,oir->oni', query_rows.astype(jnp.float32), key_rows.astype(jnp.float32)) * score_scale
    causal = jnp.arange(length)[:, None] >= jnp.arange(length)[None, :]
    score_matrix = jnp.where(causal, score_matrix, -1e+30)
    probs = jax.nn.softmax(score_matrix, axis=-1)
    probability_matrix = probs.astype(jnp.bfloat16)
    attended_output = jnp.einsum('wfx,wxh->wfh', probability_matrix.astype(jnp.float32), value_rows.astype(jnp.float32)).astype(jnp.bfloat16)
    attention_gradient = jnp.dot(grad_in.reshape(-1, width), weight[:, 3 * head:], preferred_element_type=jnp.float32)
    attention_gradient = attention_gradient.reshape(seqs, length, head).astype(jnp.bfloat16)
    probability_gradient = jnp.einsum('onr,oir->oni', attention_gradient.astype(jnp.float32), value_rows.astype(jnp.float32))
    score_gradient = probs * (probability_gradient - lax.optimization_barrier(jnp.sum(probability_gradient * probs, axis=-1, keepdims=True))) * score_scale
    score_gradient = score_gradient.astype(jnp.bfloat16).astype(jnp.float32)
    query_gradient = jnp.einsum('wfx,wxh->wfh', score_gradient, key_rows.astype(jnp.float32))
    key_gradient = jnp.einsum('cof,cod->cfd', score_gradient, query_rows.astype(jnp.float32))
    value_gradient = jnp.einsum('cof,cod->cfd', probability_matrix.astype(jnp.float32), attention_gradient.astype(jnp.float32))
    grad_proj = jnp.concatenate([unrotate(query_gradient, cosine, sine_table), unrotate(key_gradient, cosine, sine_table), value_gradient], axis=-1).astype(jnp.bfloat16)
    grad_hidden = lax.dot_general(grad_proj.reshape(-1, 3 * head), weight[:, :3 * head], (((1,), (1,)), ((), ())), preferred_element_type=jnp.float32)
    grad_hidden = grad_hidden.reshape(seqs, length, width)
    gain_term = lax.optimization_barrier(jnp.sum(grad_hidden * normed, axis=(0, 1)))
    grad_normed = grad_hidden * wide_gain
    grad_x = inv_rms * (grad_normed - normed * lax.optimization_barrier(jnp.mean(grad_normed * normed, axis=-1, keepdims=True)))
    grad_out = (grad_in.astype(jnp.float32) + grad_x).astype(jnp.bfloat16)
    return (grad_out, gain_term, hidden, grad_proj, attended_output)

def group_major(stacked):
    micro_count, seqs, length, cols = stacked.shape
    return jnp.transpose(stacked, (1, 0, 2, 3)).reshape(seqs, micro_count * length, cols)

def device_sum(hidden_all, proj_all, grad_all, att_all):
    width = hidden_all.shape[2]
    cols = proj_all.shape[2] + att_all.shape[2]

    def add_one(total, pieces):
        hid, prj, grd, att = pieces
        term = jnp.concatenate([lax.dot_general(hid, prj, (((0,), (0,)), ((), ())), preferred_element_type=jnp.float32), lax.dot_general(grd, att, (((0,), (0,)), ((), ())), preferred_element_type=jnp.float32)], axis=1)
        rounded = lax.optimization_barrier(term.astype(jnp.bfloat16))
        return (total + rounded.astype(jnp.float32), None)
    total, unused = lax.scan(add_one, jnp.zeros((width, cols), jnp.float32), (hidden_all, proj_all, grad_all, att_all))
    return total

def reference(inputs, upstream, weights, gain):
    grads = [upstream[micro].reshape(N_FSDP, TMB, D) for micro in range(MB)]
    weight_list = [None] * SECTIONS
    gain_list = [None] * SECTIONS
    for section in reversed(range(SECTIONS)):
        new_grads, gain_sum, hid_l, prj_l, grd_l, att_l = ([], jnp.zeros((D,), jnp.float32), [], [], [], [])
        for micro in range(MB):
            grad_out, gain_term, hidden, grad_proj, attended_output = section_pass(inputs[section, micro].reshape(N_FSDP, TMB, D), weights[section], gain[section], grads[micro])
            new_grads.append(grad_out)
            gain_sum = gain_sum + gain_term
            hid_l.append(hidden)
            prj_l.append(grad_proj)
            grd_l.append(grads[micro])
            att_l.append(attended_output)
        weight_list[section] = device_sum(group_major(jnp.stack(hid_l)), group_major(jnp.stack(prj_l)), group_major(jnp.stack(grd_l)), group_major(jnp.stack(att_l)))
        gain_list[section] = gain_sum
        grads = new_grads
    return (jnp.stack(weight_list), jnp.stack(gain_list))
```

```python
import jax
import jax.numpy as jnp
from jax import lax
from jax.sharding import PartitionSpec as P

F32 = jnp.float32
BF16 = jnp.bfloat16


def rope_tables(length, head):
    half_head = head // 2
    position = lax.iota(F32, length)
    freq = jnp.power(500000.0, -2.0 * lax.iota(F32, half_head) / head)
    angle = position[:, None] * freq[None, :]
    return (jnp.cos(angle), jnp.sin(angle))


def turn(rows, cos_full, sin_full):
    half = rows.shape[-1] // 2
    swapped = jnp.concatenate([rows[:, half:], rows[:, :half]], axis=-1)
    return rows * cos_full + swapped * sin_full


def dot(left, right):
    return jnp.dot(left, right, preferred_element_type=F32)


def dot_rows(left, right):
    return lax.dot_general(left, right, (((0,), (0,)), ((), ())), preferred_element_type=F32)


def dot_cols(left, right):
    return lax.dot_general(left, right, (((1,), (1,)), ((), ())), preferred_element_type=F32)


def on_device(inputs, upstream, weights, gain):
    sections = lax.axis_size("section")
    here = lax.axis_index("section")
    micro_count, length, width = inputs.shape[1:]
    head = weights.shape[2] // 4
    tokens = micro_count * length
    lower = sections - 1
    x = inputs[0].reshape(tokens, width)
    up = upstream.reshape(tokens, width)
    w_own = weights[0].astype(F32)
    gain_own = gain[0].astype(F32)[:, None]
    w_scaled = (w_own[:, : 3 * head] * gain_own).astype(BF16)
    w_back_own = weights[0][:, 3 * head :]

    w_full = lax.all_gather(
        jnp.concatenate([w_scaled, w_back_own], axis=1), "fsdp", axis=0, tiled=True
    )
    backs = lax.all_gather(w_back_own, "section", axis=0)[:lower]
    backs = jnp.transpose(backs, (1, 0, 2)).reshape(w_back_own.shape[0], lower * head)
    back_all = lax.all_gather(backs, "fsdp", axis=0, tiled=True)
    wg = w_full[:, : 3 * head]
    wb = w_full[:, 3 * head :]

    xfloat = x.astype(F32)
    inv = lax.rsqrt(jnp.mean(xfloat * xfloat, axis=1, keepdims=True) + 1e-05)
    proj = dot(x, wg) * inv
    direct = dot(up, wb)

    cosine, sine = rope_tables(length, head)
    cos_full = jnp.tile(jnp.concatenate([cosine, cosine], axis=1), (micro_count, 1))
    sin_full = jnp.tile(jnp.concatenate([-sine, sine], axis=1), (micro_count, 1))
    query = turn(proj[:, :head], cos_full, sin_full).astype(BF16)
    keys = turn(proj[:, head : 2 * head], cos_full, sin_full).astype(BF16)
    values = proj[:, 2 * head :].astype(BF16)
    scale = head ** (-0.5)
    row = lax.broadcasted_iota(jnp.int32, (tokens, tokens), 0)
    col = lax.broadcasted_iota(jnp.int32, (tokens, tokens), 1)
    seen = jnp.logical_and(row // length == col // length, row >= col)
    scores = jnp.where(seen, dot_cols(query, keys) * scale, -1e30)
    peak = jnp.max(scores, axis=1, keepdims=True)
    expd = jnp.where(seen, jnp.exp(scores - peak), 0.0)
    probs = expd / jnp.sum(expd, axis=1, keepdims=True)
    probs_b = probs.astype(BF16)
    attended = dot(probs_b, values).astype(BF16)
    att_all = lax.all_gather(attended, "section", axis=0)[:lower]
    att_all = jnp.transpose(att_all, (1, 0, 2)).reshape(tokens, lower * head)

    cross = dot_rows(wg, back_all).astype(BF16)
    through = dot(x, back_all) * inv

    def backward(grad_att):
        grad_att = grad_att.astype(BF16)
        grad_probs = dot_cols(grad_att, values)
        grad_scores = (
            probs
            * (grad_probs - jnp.sum(grad_probs * probs, axis=1, keepdims=True))
            * scale
        ).astype(BF16)
        return jnp.concatenate(
            [
                turn(dot(grad_scores, keys), cos_full, -sin_full),
                turn(dot_rows(grad_scores, query), cos_full, -sin_full),
                dot_rows(probs_b, grad_att),
            ],
            axis=1,
        ).astype(BF16)

    received = jnp.zeros((tokens, lower * head), BF16)
    own_at = jnp.minimum(here, lower - 1) * head
    for tick in range(sections):
        own = lax.dynamic_slice_in_dim(received, own_at, head, 1).astype(F32)
        own = jnp.where(here == sections - 1, 0.0, own)
        grad_proj = backward(direct + own)
        shift = jnp.sum(grad_proj.astype(F32) * proj, axis=1, keepdims=True) / width
        if tick < sections - 1:
            sent = received.astype(F32) + inv * (dot(grad_proj, cross) - shift * through)
            received = lax.ppermute(
                sent.astype(BF16), "section", [(s, s - 1) for s in range(1, sections)]
            )

    below = lax.iota(jnp.int32, lower * head)[None, :] < here * head
    att_below = jnp.where(below, att_all, jnp.zeros((), BF16))
    scaled_proj = (grad_proj.astype(F32) * inv).astype(BF16)
    scaled_att = (att_below.astype(F32) * (inv * inv * shift)).astype(BF16)
    by_x = dot_rows(x, jnp.concatenate([scaled_proj, scaled_att], axis=1))
    mixed = dot_rows(scaled_proj, att_below).astype(BF16)
    term = jnp.concatenate(
        [
            by_x[:, : 3 * head],
            dot_rows(up, attended),
            dot(wg, mixed) - by_x[:, 3 * head :],
        ],
        axis=1,
    ).astype(BF16)
    total = lax.psum_scatter(term, "fsdp", scatter_dimension=0, tiled=True)
    rows = total.shape[0]
    handed = total[:, 4 * head :].reshape(rows, lower, head)
    handed = jnp.concatenate([handed, jnp.zeros((rows, 1, head), BF16)], axis=1)
    handed = lax.psum_scatter(
        jnp.transpose(handed, (1, 0, 2)), "section", scatter_dimension=0, tiled=False
    )
    raw = total[:, : 3 * head].astype(F32)
    shard = jnp.concatenate(
        [raw * gain_own, total[:, 3 * head : 4 * head].astype(F32) + handed.astype(F32)], axis=1
    )
    gain_rows = jnp.sum(raw * w_own[:, : 3 * head], axis=1)
    gain_sum = lax.all_gather(gain_rows, "fsdp", axis=0, tiled=True)
    return (shard[None], gain_sum[None])


def solution(mesh):
    return jax.shard_map(
        on_device,
        mesh=mesh,
        in_specs=(
            P("section", None, "fsdp", None),
            P(None, "fsdp", None),
            P("section", "fsdp", None),
            P("section", "fsdp"),
        ),
        out_specs=(P("section", "fsdp", None), P("section", None)),
        check_vma=False,
    )
```

```python
import functools

import jax
import jax.numpy as jnp
from jax import lax
from jax.experimental import pallas as pl
from jax.experimental.pallas import tpu as pltpu
from jax.sharding import PartitionSpec as P

MESH = pl.DeviceIdType.MESH
VMEM_BYTES = 56 * 1024 * 1024

F32 = jnp.float32
BF16 = jnp.bfloat16


def rope_tables(length, head):
    half_head = head // 2
    position = lax.iota(F32, length)
    freq = jnp.power(500000.0, -2.0 * lax.iota(F32, half_head) / head)
    angle = position[:, None] * freq[None, :]
    return (jnp.cos(angle), jnp.sin(angle))


def turn(rows, cos_full, sin_full):
    half = rows.shape[-1] // 2
    swapped = jnp.concatenate([rows[:, half:], rows[:, :half]], axis=-1)
    return rows * cos_full + swapped * sin_full


def dot(left, right):
    return jnp.dot(left, right, preferred_element_type=F32)


def dot_rows(left, right):
    return lax.dot_general(left, right, (((0,), (0,)), ((), ())), preferred_element_type=F32)


def dot_cols(left, right):
    return lax.dot_general(left, right, (((1,), (1,)), ((), ())), preferred_element_type=F32)


def remote(src, dst, send_sem, recv_sem, section, member):
    return pltpu.make_async_remote_copy(
        src_ref=src,
        dst_ref=dst,
        send_sem=send_sem,
        recv_sem=recv_sem,
        device_id=(section, member),
        device_id_type=MESH,
    )


def greet(sections, chips, here, chip, core):
    barrier = pltpu.get_barrier_semaphore()

    def hello(section, member):
        pl.semaphore_signal(barrier, inc=1, device_id=(section, member), device_id_type=MESH)

    @pl.when(chip > 0)
    def _():
        hello(here, (chip - 1) * 2 + core)

    @pl.when(chip < chips - 1)
    def _():
        hello(here, (chip + 1) * 2 + core)

    hello(here, chip * 2 + 1 - core)

    @pl.loop(1, sections)
    def _(step):
        hello(lax.rem(here + step, sections), chip * 2 + core)

    pl.semaphore_wait(
        barrier,
        sections + (chip > 0).astype(jnp.int32) + (chip < chips - 1).astype(jnp.int32),
    )


def gather_kernel(
    sections,
    chips,
    w_ref,
    x_ref,
    up_ref,
    full,
    proj,
    through,
    cross,
    back,
    z_recv,
    z_right,
    z_left,
    sib_recv,
    sib_send,
    x_recv,
    x_send,
    sibx_recv,
    sibx_send,
):
    here = lax.axis_index("section")
    member = lax.axis_index("fsdp")
    chip = member // 2
    core = member % 2
    sibling = chip * 2 + 1 - core
    rows = w_ref.shape[0]
    head = w_ref.shape[1] // 4
    full[member] = w_ref[...]
    proj[...] = jnp.zeros_like(proj)
    through[...] = jnp.zeros_like(through)
    cross[...] = jnp.zeros_like(cross)
    greet(sections, chips, here, chip, core)

    def to_right(b):
        block = full.at[b * 2 + core]
        return remote(block, block, z_right.at[b], z_recv.at[b], here, member + 2)

    def to_left(b):
        block = full.at[b * 2 + core]
        return remote(block, block, z_left.at[b], z_recv.at[b], here, member - 2)

    def to_sibling(b, lane):
        block = full.at[b * 2 + lane]
        return remote(block, block, sib_send.at[b], sib_recv.at[b], here, sibling)

    def to_section(b, source, section):
        return remote(
            full.at[b * 2 + core, :, pl.ds(3 * head, head)],
            back.at[source, b * 2 + core],
            x_send.at[section, b],
            x_recv.at[source, b],
            section,
            member,
        )

    def back_to_sibling(b, source, lane):
        block = back.at[source, b * 2 + lane]
        return remote(
            block, block, sibx_send.at[source, b], sibx_recv.at[source, b], here, sibling
        )

    def columns(idx):
        return pl.ds(pl.multiple_of(idx * rows, rows), rows)

    def products(idx):
        proj[:, : 3 * head] += dot(x_ref[:, columns(idx)], full[idx, :, : 3 * head])
        proj[:, 3 * head :] += dot(up_ref[:, columns(idx)], full[idx, :, 3 * head :])

    def back_products(source, idx):
        through[source] += dot(x_ref[:, columns(idx)], back[source, idx])
        cross[source] += dot_rows(full[idx, :, : 3 * head], back[source, idx])

    def arrived(b):
        @pl.when(b < chip)
        def _():
            to_right(b).wait_recv()

        @pl.when(b > chip)
        def _():
            to_left(b).wait_recv()

        @pl.when(jnp.logical_and(b <= chip, chip < chips - 1))
        def _():
            to_right(b).start()

        @pl.when(jnp.logical_and(b >= chip, chip > 0))
        def _():
            to_left(b).start()

        to_sibling(b, core).start()

        @pl.loop(here + 1, sections)
        def _(section):
            to_section(b, here, section).start()

        products(b * 2 + core)

    def second(b):
        to_sibling(b, 1 - core).wait_recv()
        products(b * 2 + 1 - core)

        @pl.loop(0, here)
        def _(source):
            to_section(b, source, here).wait_recv()
            back_to_sibling(b, source, core).start()
            back_products(source, b * 2 + core)

    def third(b):
        @pl.loop(0, here)
        def _(source):
            back_to_sibling(b, source, 1 - core).wait_recv()
            back_products(source, b * 2 + 1 - core)

    def done(b):
        @pl.when(jnp.logical_and(b <= chip, chip < chips - 1))
        def _():
            to_right(b).wait_send()

        @pl.when(jnp.logical_and(b >= chip, chip > 0))
        def _():
            to_left(b).wait_send()

        to_sibling(b, core).wait_send()

        @pl.loop(here + 1, sections)
        def _(section):
            to_section(b, here, section).wait_send()

        @pl.loop(0, here)
        def _(source):
            back_to_sibling(b, source, core).wait_send()

    @pl.loop(0, 2 * (chips + 2))
    def _(turn_no):
        side = turn_no % 2
        for lag, act in enumerate((arrived, second, third)):
            away = turn_no // 2 - lag
            b = jnp.where(side == 1, chip + away, chip - away)
            first = jnp.where(side == 1, 1, 0)
            fits = jnp.logical_and(b >= 0, b < chips)
            pl.when(jnp.logical_and(fits, away >= first))(functools.partial(act, b))

    pl.loop(0, chips)(done)


def gathered(sections, members, w_rows, x, up):
    rows, cols = w_rows.shape
    head = cols // 4
    tokens = x.shape[0]
    chips = members // 2
    lower = sections - 1
    vmem = pl.BlockSpec(memory_space=pltpu.VMEM)
    dma = pltpu.SemaphoreType.DMA
    return pl.pallas_call(
        functools.partial(gather_kernel, sections, chips),
        out_shape=(
            jax.ShapeDtypeStruct((members, rows, cols), BF16),
            jax.ShapeDtypeStruct((tokens, cols), F32),
            jax.ShapeDtypeStruct((lower, tokens, head), F32),
            jax.ShapeDtypeStruct((lower, 3 * head, head), F32),
        ),
        in_specs=[vmem] * 3,
        out_specs=(vmem,) * 4,
        scratch_shapes=[
            pltpu.VMEM((lower, members, rows, head), BF16),
            dma((chips,)),
            dma((chips,)),
            dma((chips,)),
            dma((chips,)),
            dma((chips,)),
            dma((lower, chips)),
            dma((sections, chips)),
            dma((lower, chips)),
            dma((lower, chips)),
        ],
        compiler_params=pltpu.CompilerParams(
            collective_id=0, has_side_effects=True, vmem_limit_bytes=VMEM_BYTES
        ),
        cost_estimate=pl.CostEstimate(
            flops=2 * tokens * members * rows * cols, bytes_accessed=1 << 23, transcendentals=0
        ),
    )(w_rows, x, up)


def on_device(inputs, upstream, weights, gain):
    sections = lax.axis_size("section")
    here = lax.axis_index("section")
    micro_count, length, width = inputs.shape[1:]
    head = weights.shape[2] // 4
    tokens = micro_count * length
    lower = sections - 1
    x = inputs[0].reshape(tokens, width)
    up = upstream.reshape(tokens, width)
    w_own = weights[0].astype(F32)
    gain_own = gain[0].astype(F32)[:, None]
    w_scaled = (w_own[:, : 3 * head] * gain_own).astype(BF16)
    w_back_own = weights[0][:, 3 * head :]

    members = lax.axis_size("fsdp")
    full, products, through, cross = gathered(
        sections, members, jnp.concatenate([w_scaled, w_back_own], axis=1), x, up
    )
    wg = full.reshape(width, 4 * head)[:, : 3 * head]
    xfloat = x.astype(F32)
    inv = lax.rsqrt(jnp.mean(xfloat * xfloat, axis=1, keepdims=True) + 1e-05)
    proj = products[:, : 3 * head] * inv
    direct = products[:, 3 * head :]

    cosine, sine = rope_tables(length, head)
    cos_full = jnp.tile(jnp.concatenate([cosine, cosine], axis=1), (micro_count, 1))
    sin_full = jnp.tile(jnp.concatenate([-sine, sine], axis=1), (micro_count, 1))
    query = turn(proj[:, :head], cos_full, sin_full).astype(BF16)
    keys = turn(proj[:, head : 2 * head], cos_full, sin_full).astype(BF16)
    values = proj[:, 2 * head :].astype(BF16)
    scale = head ** (-0.5)
    row = lax.broadcasted_iota(jnp.int32, (tokens, tokens), 0)
    col = lax.broadcasted_iota(jnp.int32, (tokens, tokens), 1)
    seen = jnp.logical_and(row // length == col // length, row >= col)
    scores = jnp.where(seen, dot_cols(query, keys) * scale, -1e30)
    peak = jnp.max(scores, axis=1, keepdims=True)
    expd = jnp.where(seen, jnp.exp(scores - peak), 0.0)
    probs = expd / jnp.sum(expd, axis=1, keepdims=True)
    probs_b = probs.astype(BF16)
    attended = dot(probs_b, values).astype(BF16)
    att_all = lax.all_gather(attended, "section", axis=0)[:lower]
    att_all = jnp.transpose(att_all, (1, 0, 2)).reshape(tokens, lower * head)

    cross = jnp.transpose(cross, (1, 0, 2)).reshape(3 * head, lower * head).astype(BF16)
    through = jnp.transpose(through, (1, 0, 2)).reshape(tokens, lower * head) * inv

    def backward(grad_att):
        grad_att = grad_att.astype(BF16)
        grad_probs = dot_cols(grad_att, values)
        grad_scores = (
            probs
            * (grad_probs - jnp.sum(grad_probs * probs, axis=1, keepdims=True))
            * scale
        ).astype(BF16)
        return jnp.concatenate(
            [
                turn(dot(grad_scores, keys), cos_full, -sin_full),
                turn(dot_rows(grad_scores, query), cos_full, -sin_full),
                dot_rows(probs_b, grad_att),
            ],
            axis=1,
        ).astype(BF16)

    received = jnp.zeros((tokens, lower * head), BF16)
    own_at = jnp.minimum(here, lower - 1) * head
    for tick in range(sections):
        own = lax.dynamic_slice_in_dim(received, own_at, head, 1).astype(F32)
        own = jnp.where(here == sections - 1, 0.0, own)
        grad_proj = backward(direct + own)
        shift = jnp.sum(grad_proj.astype(F32) * proj, axis=1, keepdims=True) / width
        if tick < sections - 1:
            sent = received.astype(F32) + inv * (dot(grad_proj, cross) - shift * through)
            received = lax.ppermute(
                sent.astype(BF16), "section", [(s, s - 1) for s in range(1, sections)]
            )

    below = lax.iota(jnp.int32, lower * head)[None, :] < here * head
    att_below = jnp.where(below, att_all, jnp.zeros((), BF16))
    scaled_proj = (grad_proj.astype(F32) * inv).astype(BF16)
    scaled_att = (att_below.astype(F32) * (inv * inv * shift)).astype(BF16)
    by_x = dot_rows(x, jnp.concatenate([scaled_proj, scaled_att], axis=1))
    mixed = dot_rows(scaled_proj, att_below).astype(BF16)
    term = jnp.concatenate(
        [
            by_x[:, : 3 * head],
            dot_rows(up, attended),
            dot(wg, mixed) - by_x[:, 3 * head :],
        ],
        axis=1,
    ).astype(BF16)
    total = lax.psum_scatter(term, "fsdp", scatter_dimension=0, tiled=True)
    rows = total.shape[0]
    handed = total[:, 4 * head :].reshape(rows, lower, head)
    handed = jnp.concatenate([handed, jnp.zeros((rows, 1, head), BF16)], axis=1)
    handed = lax.psum_scatter(
        jnp.transpose(handed, (1, 0, 2)), "section", scatter_dimension=0, tiled=False
    )
    raw = total[:, : 3 * head].astype(F32)
    shard = jnp.concatenate(
        [raw * gain_own, total[:, 3 * head : 4 * head].astype(F32) + handed.astype(F32)], axis=1
    )
    gain_rows = jnp.sum(raw * w_own[:, : 3 * head], axis=1)
    gain_sum = lax.all_gather(gain_rows, "fsdp", axis=0, tiled=True)
    return (shard[None], gain_sum[None])


def solution(mesh):
    return jax.shard_map(
        on_device,
        mesh=mesh,
        in_specs=(
            P("section", None, "fsdp", None),
            P(None, "fsdp", None),
            P("section", "fsdp", None),
            P("section", "fsdp"),
        ),
        out_specs=(P("section", "fsdp", None), P("section", None)),
        check_vma=False,
    )
```

```python
import functools

import jax
import jax.numpy as jnp
from jax import lax
from jax.experimental import pallas as pl
from jax.experimental.pallas import tpu as pltpu
from jax.sharding import PartitionSpec as P

MESH = pl.DeviceIdType.MESH
VMEM_BYTES = 56 * 1024 * 1024

F32 = jnp.float32
BF16 = jnp.bfloat16


def rope_tables(length, head):
    half_head = head // 2
    position = lax.iota(F32, length)
    freq = jnp.power(500000.0, -2.0 * lax.iota(F32, half_head) / head)
    angle = position[:, None] * freq[None, :]
    return (jnp.cos(angle), jnp.sin(angle))


def turn(rows, cos_full, sin_full):
    half = rows.shape[-1] // 2
    swapped = jnp.concatenate([rows[:, half:], rows[:, :half]], axis=-1)
    return rows * cos_full + swapped * sin_full


def dot(left, right):
    return jnp.dot(left, right, preferred_element_type=F32)


def dot_rows(left, right):
    return lax.dot_general(left, right, (((0,), (0,)), ((), ())), preferred_element_type=F32)


def dot_cols(left, right):
    return lax.dot_general(left, right, (((1,), (1,)), ((), ())), preferred_element_type=F32)


def remote(src, dst, send_sem, recv_sem, section, member):
    return pltpu.make_async_remote_copy(
        src_ref=src,
        dst_ref=dst,
        send_sem=send_sem,
        recv_sem=recv_sem,
        device_id=(section, member),
        device_id_type=MESH,
    )


def greet(sections, chips, here, chip, core):
    barrier = pltpu.get_barrier_semaphore()

    def hello(section, member):
        pl.semaphore_signal(barrier, inc=1, device_id=(section, member), device_id_type=MESH)

    @pl.when(chip > 0)
    def _():
        hello(here, (chip - 1) * 2 + core)

    @pl.when(chip < chips - 1)
    def _():
        hello(here, (chip + 1) * 2 + core)

    hello(here, chip * 2 + 1 - core)

    @pl.loop(1, sections)
    def _(step):
        hello(lax.rem(here + step, sections), chip * 2 + core)

    pl.semaphore_wait(
        barrier,
        sections + (chip > 0).astype(jnp.int32) + (chip < chips - 1).astype(jnp.int32),
    )


def gather_kernel(
    sections,
    chips,
    w_ref,
    x_ref,
    up_ref,
    full,
    proj,
    through,
    cross,
    back,
    z_recv,
    z_right,
    z_left,
    sib_recv,
    sib_send,
    x_recv,
    x_send,
    sibx_recv,
    sibx_send,
):
    here = lax.axis_index("section")
    member = lax.axis_index("fsdp")
    chip = member // 2
    core = member % 2
    sibling = chip * 2 + 1 - core
    rows = w_ref.shape[0]
    head = w_ref.shape[1] // 4
    full[member] = w_ref[...]
    proj[...] = jnp.zeros_like(proj)
    through[...] = jnp.zeros_like(through)
    cross[...] = jnp.zeros_like(cross)
    greet(sections, chips, here, chip, core)

    def to_right(b):
        block = full.at[b * 2 + core]
        return remote(block, block, z_right.at[b], z_recv.at[b], here, member + 2)

    def to_left(b):
        block = full.at[b * 2 + core]
        return remote(block, block, z_left.at[b], z_recv.at[b], here, member - 2)

    def to_sibling(b, lane):
        block = full.at[b * 2 + lane]
        return remote(block, block, sib_send.at[b], sib_recv.at[b], here, sibling)

    def to_section(b, source, section):
        return remote(
            full.at[b * 2 + core, :, pl.ds(3 * head, head)],
            back.at[source, b * 2 + core],
            x_send.at[section, b],
            x_recv.at[source, b],
            section,
            member,
        )

    def back_to_sibling(b, source, lane):
        block = back.at[source, b * 2 + lane]
        return remote(
            block, block, sibx_send.at[source, b], sibx_recv.at[source, b], here, sibling
        )

    def columns(idx):
        return pl.ds(pl.multiple_of(idx * rows, rows), rows)

    def products(idx):
        proj[:, : 3 * head] += dot(x_ref[:, columns(idx)], full[idx, :, : 3 * head])
        proj[:, 3 * head :] += dot(up_ref[:, columns(idx)], full[idx, :, 3 * head :])

    def back_products(source, idx):
        through[source] += dot(x_ref[:, columns(idx)], back[source, idx])
        cross[source] += dot_rows(full[idx, :, : 3 * head], back[source, idx])

    def arrived(b):
        @pl.when(b < chip)
        def _():
            to_right(b).wait_recv()

        @pl.when(b > chip)
        def _():
            to_left(b).wait_recv()

        @pl.when(jnp.logical_and(b <= chip, chip < chips - 1))
        def _():
            to_right(b).start()

        @pl.when(jnp.logical_and(b >= chip, chip > 0))
        def _():
            to_left(b).start()

        to_sibling(b, core).start()

        @pl.loop(here + 1, sections)
        def _(section):
            to_section(b, here, section).start()

        products(b * 2 + core)

    def second(b):
        to_sibling(b, 1 - core).wait_recv()
        products(b * 2 + 1 - core)

        @pl.loop(0, here)
        def _(source):
            to_section(b, source, here).wait_recv()
            back_to_sibling(b, source, core).start()
            back_products(source, b * 2 + core)

    def third(b):
        @pl.loop(0, here)
        def _(source):
            back_to_sibling(b, source, 1 - core).wait_recv()
            back_products(source, b * 2 + 1 - core)

    def done(b):
        @pl.when(jnp.logical_and(b <= chip, chip < chips - 1))
        def _():
            to_right(b).wait_send()

        @pl.when(jnp.logical_and(b >= chip, chip > 0))
        def _():
            to_left(b).wait_send()

        to_sibling(b, core).wait_send()

        @pl.loop(here + 1, sections)
        def _(section):
            to_section(b, here, section).wait_send()

        @pl.loop(0, here)
        def _(source):
            back_to_sibling(b, source, core).wait_send()

    @pl.loop(0, 2 * (chips + 2))
    def _(turn_no):
        side = turn_no % 2
        for lag, act in enumerate((arrived, second, third)):
            away = turn_no // 2 - lag
            b = jnp.where(side == 1, chip + away, chip - away)
            first = jnp.where(side == 1, 1, 0)
            fits = jnp.logical_and(b >= 0, b < chips)
            pl.when(jnp.logical_and(fits, away >= first))(functools.partial(act, b))

    pl.loop(0, chips)(done)


def gathered(sections, members, w_rows, x, up):
    rows, cols = w_rows.shape
    head = cols // 4
    tokens = x.shape[0]
    chips = members // 2
    lower = sections - 1
    vmem = pl.BlockSpec(memory_space=pltpu.VMEM)
    dma = pltpu.SemaphoreType.DMA
    return pl.pallas_call(
        functools.partial(gather_kernel, sections, chips),
        out_shape=(
            jax.ShapeDtypeStruct((members, rows, cols), BF16),
            jax.ShapeDtypeStruct((tokens, cols), F32),
            jax.ShapeDtypeStruct((lower, tokens, head), F32),
            jax.ShapeDtypeStruct((lower, 3 * head, head), F32),
        ),
        in_specs=[vmem] * 3,
        out_specs=(vmem,) * 4,
        scratch_shapes=[
            pltpu.VMEM((lower, members, rows, head), BF16),
            dma((chips,)),
            dma((chips,)),
            dma((chips,)),
            dma((chips,)),
            dma((chips,)),
            dma((lower, chips)),
            dma((sections, chips)),
            dma((lower, chips)),
            dma((lower, chips)),
        ],
        compiler_params=pltpu.CompilerParams(
            collective_id=0, has_side_effects=True, vmem_limit_bytes=VMEM_BYTES
        ),
        cost_estimate=pl.CostEstimate(
            flops=2 * tokens * members * rows * cols, bytes_accessed=1 << 23, transcendentals=0
        ),
    )(w_rows, x, up)


def scatter_kernel(
    sections,
    chips,
    x_ref,
    up_ref,
    full,
    own_rhs,
    low_rhs,
    mixed,
    att,
    w_ref,
    gain_ref,
    out,
    gains,
    acc,
    sib_out,
    sib_in,
    sibx_out,
    sibx_in,
    x_in,
    z_out,
    z_in,
    sib_send,
    sib_recv,
    sibx_send,
    sibx_recv,
    x_send,
    x_recv,
    z_send,
    z_recv,
    g_send,
    g_recv,
):
    here = lax.axis_index("section")
    member = lax.axis_index("fsdp")
    members = 2 * chips
    chip = member // 2
    core = member % 2
    sibling = chip * 2 + 1 - core
    rows = w_ref.shape[0]
    head = w_ref.shape[1] // 4
    wide = pl.ds(0, 3 * head)
    last = pl.ds(3 * head, head)

    barrier = pltpu.get_barrier_semaphore()

    @pl.loop(1, sections)
    def _(step):
        pl.semaphore_signal(
            barrier,
            inc=1,
            device_id=(lax.rem(here + step, sections), member),
            device_id_type=MESH,
        )

    @pl.loop(1, members)
    def _(step):
        pl.semaphore_signal(
            barrier, inc=1, device_id=(here, lax.rem(member + step, members)), device_id_type=MESH
        )

    pl.semaphore_wait(barrier, sections - 1 + members - 1)

    def columns(idx):
        return pl.ds(pl.multiple_of(idx * rows, rows), rows)

    def to_sibling(b):
        return remote(sib_out.at[b], sib_in.at[b], sib_send.at[b], sib_recv.at[b], here, sibling)

    def low_to_sibling(b, target):
        return remote(
            sibx_out.at[target, b],
            sibx_in.at[target, b],
            sibx_send.at[target, b],
            sibx_recv.at[target, b],
            here,
            sibling,
        )

    def to_section(b, source, target):
        return remote(
            sibx_in.at[target, b],
            x_in.at[source - 1, b],
            x_send.at[target, b],
            x_recv.at[source - 1, b],
            target,
            member,
        )

    def hop(b, part, side):
        cols = last if part else wide
        return remote(
            z_out.at[b, :, cols],
            z_in.at[side, b, :, cols],
            z_send.at[part, b],
            z_recv.at[part, side, b],
            here,
            member - 2 if side else member + 2,
        )

    def gain_to(other):
        return remote(
            gains.at[member], gains.at[member], g_send.at[other], g_recv.at[member], here, other
        )

    def gain_from(other):
        return remote(
            gains.at[other], gains.at[other], g_send.at[other], g_recv.at[other], here, other
        )

    def for_lower(idx, target):
        return dot(full[idx, :, wide], mixed[target]) - dot_rows(
            x_ref[:, columns(idx)], low_rhs[target]
        )

    def far_first(act):
        @pl.loop(0, 2 * chips)
        def _(turn_no):
            side = turn_no % 2
            away = turn_no // 2
            b = jnp.where(side == 1, away, chips - 1 - away)
            fits = jnp.where(side == 1, jnp.where(b < chip, 1, 0), jnp.where(b > chip, 1, 0))

            @pl.when(fits == 1)
            def _():
                act(b)

        act(chip)

    def for_sibling(b):
        idx = b * 2 + 1 - core

        @pl.loop(0, here)
        def _(target):
            sibx_out[target, b] = for_lower(idx, target).astype(BF16)
            low_to_sibling(b, target).start()

        sib_out[b, :, wide] = dot_rows(x_ref[:, columns(idx)], own_rhs[...]).astype(BF16)
        sib_out[b, :, last] = dot_rows(up_ref[:, columns(idx)], att[...]).astype(BF16)
        to_sibling(b).start()

    def for_sections(b):
        @pl.loop(0, here)
        def _(target):
            mine = for_lower(b * 2 + core, target)
            low_to_sibling(b, target).wait_recv()
            both = mine + sibx_in[target, b].astype(F32)
            sibx_in[target, b] = both.astype(BF16)
            to_section(b, here, target).start()

    def along(b, part):
        cols = last if part else wide

        @pl.when(jnp.logical_and(b >= chip, chip > 0))
        def _():
            hop(b, part, 0).wait_recv()
            acc[:, cols] += z_in[0, b, :, cols].astype(F32)

        @pl.when(jnp.logical_and(b <= chip, chip < chips - 1))
        def _():
            hop(b, part, 1).wait_recv()
            acc[:, cols] += z_in[1, b, :, cols].astype(F32)

        @pl.when(b != chip)
        def _():
            z_out[b, :, cols] = acc[:, cols].astype(BF16)

        @pl.when(b > chip)
        def _():
            hop(b, part, 0).start()

        @pl.when(b < chip)
        def _():
            hop(b, part, 1).start()

    def first_part(b):
        mine = dot_rows(x_ref[:, columns(b * 2 + core)], own_rhs[...])
        to_sibling(b).wait_recv()
        acc[:, wide] = mine + sib_in[b, :, wide].astype(F32)
        along(b, 0)

    def second_part(b):
        acc[:, last] = dot_rows(up_ref[:, columns(b * 2 + core)], att[...]) + sib_in[
            b, :, last
        ].astype(F32)

        @pl.loop(here + 1, sections)
        def _(source):
            to_section(b, source, here).wait_recv()
            acc[:, last] += x_in[source - 1, b].astype(F32)

        along(b, 1)

    far_first(for_sibling)
    far_first(for_sections)
    far_first(first_part)

    raw = acc[:, wide]
    out[:, wide] = raw * gain_ref[...]
    gain_rows = jnp.sum(raw * w_ref[:, wide].astype(F32), axis=1, keepdims=True)
    gains[member] = jnp.transpose(jnp.broadcast_to(gain_rows, (rows, 128)))[:8]

    @pl.loop(1, members)
    def _(step):
        gain_to(lax.rem(member + step, members)).start()

    far_first(second_part)
    out[:, last] = acc[:, last]

    @pl.loop(0, chips)
    def _(b):
        to_sibling(b).wait_send()

        @pl.loop(0, here)
        def _(target):
            low_to_sibling(b, target).wait_send()
            to_section(b, here, target).wait_send()

        @pl.when(b != chip)
        def _():
            hop(b, 0, 0).wait_send()
            hop(b, 1, 0).wait_send()

    @pl.loop(1, members)
    def _(step):
        other = lax.rem(member + step, members)
        gain_from(other).wait_recv()
        gain_to(other).wait_send()


def scattered(sections, members, x, up, full, own_rhs, low_rhs, mixed, att, w_own, gain_col):
    rows, cols = w_own.shape
    head = cols // 4
    chips = members // 2
    lower = sections - 1
    vmem = pl.BlockSpec(memory_space=pltpu.VMEM)
    dma = pltpu.SemaphoreType.DMA
    return pl.pallas_call(
        functools.partial(scatter_kernel, sections, chips),
        out_shape=(
            jax.ShapeDtypeStruct((rows, cols), F32),
            jax.ShapeDtypeStruct((members, 8, rows), F32),
        ),
        in_specs=[vmem] * 9,
        out_specs=(vmem,) * 2,
        scratch_shapes=[
            pltpu.VMEM((rows, cols), F32),
            pltpu.VMEM((chips, rows, cols), BF16),
            pltpu.VMEM((chips, rows, cols), BF16),
            pltpu.VMEM((lower, chips, rows, head), BF16),
            pltpu.VMEM((lower, chips, rows, head), BF16),
            pltpu.VMEM((lower, chips, rows, head), BF16),
            pltpu.VMEM((chips, rows, cols), BF16),
            pltpu.VMEM((2, chips, rows, cols), BF16),
            dma((chips,)),
            dma((chips,)),
            dma((lower, chips)),
            dma((lower, chips)),
            dma((lower, chips)),
            dma((lower, chips)),
            dma((2, chips)),
            dma((2, 2, chips)),
            dma((members,)),
            dma((members,)),
        ],
        compiler_params=pltpu.CompilerParams(
            collective_id=1, has_side_effects=True, vmem_limit_bytes=VMEM_BYTES
        ),
        cost_estimate=pl.CostEstimate(
            flops=2 * x.size * cols, bytes_accessed=1 << 23, transcendentals=0
        ),
    )(x, up, full, own_rhs, low_rhs, mixed, att, w_own, gain_col)


def on_device(inputs, upstream, weights, gain):
    sections = lax.axis_size("section")
    here = lax.axis_index("section")
    micro_count, length, width = inputs.shape[1:]
    head = weights.shape[2] // 4
    tokens = micro_count * length
    lower = sections - 1
    x = inputs[0].reshape(tokens, width)
    up = upstream.reshape(tokens, width)
    w_own = weights[0].astype(F32)
    gain_own = gain[0].astype(F32)[:, None]
    w_scaled = (w_own[:, : 3 * head] * gain_own).astype(BF16)
    w_back_own = weights[0][:, 3 * head :]

    members = lax.axis_size("fsdp")
    full, products, through, cross = gathered(
        sections, members, jnp.concatenate([w_scaled, w_back_own], axis=1), x, up
    )
    xfloat = x.astype(F32)
    inv = lax.rsqrt(jnp.mean(xfloat * xfloat, axis=1, keepdims=True) + 1e-05)
    proj = products[:, : 3 * head] * inv
    direct = products[:, 3 * head :]

    cosine, sine = rope_tables(length, head)
    cos_full = jnp.tile(jnp.concatenate([cosine, cosine], axis=1), (micro_count, 1))
    sin_full = jnp.tile(jnp.concatenate([-sine, sine], axis=1), (micro_count, 1))
    query = turn(proj[:, :head], cos_full, sin_full).astype(BF16)
    keys = turn(proj[:, head : 2 * head], cos_full, sin_full).astype(BF16)
    values = proj[:, 2 * head :].astype(BF16)
    scale = head ** (-0.5)
    row = lax.broadcasted_iota(jnp.int32, (tokens, tokens), 0)
    col = lax.broadcasted_iota(jnp.int32, (tokens, tokens), 1)
    seen = jnp.logical_and(row // length == col // length, row >= col)
    scores = jnp.where(seen, dot_cols(query, keys) * scale, -1e30)
    peak = jnp.max(scores, axis=1, keepdims=True)
    expd = jnp.where(seen, jnp.exp(scores - peak), 0.0)
    probs = expd / jnp.sum(expd, axis=1, keepdims=True)
    probs_b = probs.astype(BF16)
    attended = dot(probs_b, values).astype(BF16)
    att_all = lax.all_gather(attended, "section", axis=0)[:lower]
    att_all = jnp.transpose(att_all, (1, 0, 2)).reshape(tokens, lower * head)

    cross = jnp.transpose(cross, (1, 0, 2)).reshape(3 * head, lower * head).astype(BF16)
    through = jnp.transpose(through, (1, 0, 2)).reshape(tokens, lower * head) * inv

    def backward(grad_att):
        grad_att = grad_att.astype(BF16)
        grad_probs = dot_cols(grad_att, values)
        grad_scores = (
            probs
            * (grad_probs - jnp.sum(grad_probs * probs, axis=1, keepdims=True))
            * scale
        ).astype(BF16)
        return jnp.concatenate(
            [
                turn(dot(grad_scores, keys), cos_full, -sin_full),
                turn(dot_rows(grad_scores, query), cos_full, -sin_full),
                dot_rows(probs_b, grad_att),
            ],
            axis=1,
        ).astype(BF16)

    received = jnp.zeros((tokens, lower * head), BF16)
    own_at = jnp.minimum(here, lower - 1) * head
    for tick in range(sections):
        own = lax.dynamic_slice_in_dim(received, own_at, head, 1).astype(F32)
        own = jnp.where(here == sections - 1, 0.0, own)
        grad_proj = backward(direct + own)
        shift = jnp.sum(grad_proj.astype(F32) * proj, axis=1, keepdims=True) / width
        if tick < sections - 1:
            sent = received.astype(F32) + inv * (dot(grad_proj, cross) - shift * through)
            received = lax.ppermute(
                sent.astype(BF16), "section", [(s, s - 1) for s in range(1, sections)]
            )

    below = lax.iota(jnp.int32, lower * head)[None, :] < here * head
    att_below = jnp.where(below, att_all, jnp.zeros((), BF16))
    scaled_proj = (grad_proj.astype(F32) * inv).astype(BF16)
    scaled_att = (att_below.astype(F32) * (inv * inv * shift)).astype(BF16)
    mixed = dot_rows(scaled_proj, att_below).astype(BF16)

    def by_layer(value):
        return jnp.transpose(value.reshape(value.shape[0], lower, head), (1, 0, 2))

    shard, gains = scattered(
        sections,
        members,
        x,
        up,
        full,
        scaled_proj,
        by_layer(scaled_att),
        by_layer(mixed),
        attended,
        weights[0],
        gain_own,
    )
    return (shard[None], gains[:, 0, :].reshape(1, width))


def solution(mesh):
    return jax.shard_map(
        on_device,
        mesh=mesh,
        in_specs=(
            P("section", None, "fsdp", None),
            P(None, "fsdp", None),
            P("section", "fsdp", None),
            P("section", "fsdp"),
        ),
        out_specs=(P("section", "fsdp", None), P("section", None)),
        check_vma=False,
    )
```

```python
import functools

import jax
import jax.numpy as jnp
from jax import lax
from jax.experimental import pallas as pl
from jax.experimental.pallas import tpu as pltpu
from jax.sharding import PartitionSpec as P

MESH = pl.DeviceIdType.MESH
VMEM_BYTES = 56 * 1024 * 1024

F32 = jnp.float32
BF16 = jnp.bfloat16


def rope_tables(length, head):
    half_head = head // 2
    position = lax.iota(F32, length)
    freq = jnp.power(500000.0, -2.0 * lax.iota(F32, half_head) / head)
    angle = position[:, None] * freq[None, :]
    return (jnp.cos(angle), jnp.sin(angle))


def turn(rows, cos_full, sin_full):
    return rows * cos_full + pltpu.roll(rows, rows.shape[-1] // 2, 1) * sin_full


def dot(left, right):
    return jnp.dot(left, right, preferred_element_type=F32)


def dot_rows(left, right):
    return lax.dot_general(left, right, (((0,), (0,)), ((), ())), preferred_element_type=F32)


def dot_cols(left, right):
    return lax.dot_general(left, right, (((1,), (1,)), ((), ())), preferred_element_type=F32)


def remote(src, dst, send_sem, recv_sem, section, member):
    return pltpu.make_async_remote_copy(
        src_ref=src,
        dst_ref=dst,
        send_sem=send_sem,
        recv_sem=recv_sem,
        device_id=(section, member),
        device_id_type=MESH,
    )


def greet(sections, chips, here, chip, core):
    barrier = pltpu.get_barrier_semaphore()

    def hello(section, member):
        pl.semaphore_signal(barrier, inc=1, device_id=(section, member), device_id_type=MESH)

    @pl.when(chip > 0)
    def _():
        hello(here, (chip - 1) * 2 + core)

    @pl.when(chip < chips - 1)
    def _():
        hello(here, (chip + 1) * 2 + core)

    hello(here, chip * 2 + 1 - core)

    @pl.loop(1, sections)
    def _(step):
        hello(lax.rem(here + step, sections), chip * 2 + core)

    pl.semaphore_wait(
        barrier,
        sections + (chip > 0).astype(jnp.int32) + (chip < chips - 1).astype(jnp.int32),
    )


def gather_kernel(
    sections,
    chips,
    w_ref,
    x_ref,
    up_ref,
    cos_ref,
    sin_ref,
    keep_ref,
    full,
    own_rhs,
    low_rhs,
    mixed,
    att,
    proj,
    squares,
    through,
    cross,
    back,
    att_in,
    c_out,
    c_in,
    z_recv,
    z_right,
    z_left,
    sib_recv,
    sib_send,
    x_recv,
    x_send,
    sibx_recv,
    sibx_send,
    att_send,
    att_recv,
    c_send,
    c_recv,
):
    here = lax.axis_index("section")
    member = lax.axis_index("fsdp")
    chip = member // 2
    core = member % 2
    sibling = chip * 2 + 1 - core
    rows = w_ref.shape[0]
    head = w_ref.shape[1] // 4
    full[member] = w_ref[...]
    proj[...] = jnp.zeros_like(proj)
    squares[...] = jnp.zeros_like(squares)
    through[...] = jnp.zeros_like(through)
    cross[...] = jnp.zeros_like(cross)
    greet(sections, chips, here, chip, core)

    def to_right(b):
        block = full.at[b * 2 + core]
        return remote(block, block, z_right.at[b], z_recv.at[b], here, member + 2)

    def to_left(b):
        block = full.at[b * 2 + core]
        return remote(block, block, z_left.at[b], z_recv.at[b], here, member - 2)

    def to_sibling(b, lane):
        block = full.at[b * 2 + lane]
        return remote(block, block, sib_send.at[b], sib_recv.at[b], here, sibling)

    def to_section(b, source, section):
        return remote(
            full.at[b * 2 + core, :, pl.ds(3 * head, head)],
            back.at[source, b * 2 + core],
            x_send.at[section, b],
            x_recv.at[source, b],
            section,
            member,
        )

    def back_to_sibling(b, source, lane):
        block = back.at[source, b * 2 + lane]
        return remote(
            block, block, sibx_send.at[source, b], sibx_recv.at[source, b], here, sibling
        )

    def columns(idx):
        return pl.ds(pl.multiple_of(idx * rows, rows), rows)

    def products(idx):
        wide = x_ref[:, columns(idx)].astype(F32)
        squares[...] += jnp.sum(wide * wide, axis=1, keepdims=True)
        proj[:, : 3 * head] += dot(x_ref[:, columns(idx)], full[idx, :, : 3 * head])
        proj[:, 3 * head :] += dot(up_ref[:, columns(idx)], full[idx, :, 3 * head :])

    def back_products(source, idx):
        through[source] += dot(x_ref[:, columns(idx)], back[source, idx])
        cross[source] += dot_rows(full[idx, :, : 3 * head], back[source, idx])

    def arrived(b):
        @pl.when(b < chip)
        def _():
            to_right(b).wait_recv()

        @pl.when(b > chip)
        def _():
            to_left(b).wait_recv()

        @pl.when(jnp.logical_and(b <= chip, chip < chips - 1))
        def _():
            to_right(b).start()

        @pl.when(jnp.logical_and(b >= chip, chip > 0))
        def _():
            to_left(b).start()

        to_sibling(b, core).start()

        @pl.loop(here + 1, sections)
        def _(section):
            to_section(b, here, section).start()

        products(b * 2 + core)

    def second(b):
        to_sibling(b, 1 - core).wait_recv()
        products(b * 2 + 1 - core)

        @pl.loop(0, here)
        def _(source):
            to_section(b, source, here).wait_recv()
            back_to_sibling(b, source, core).start()
            back_products(source, b * 2 + core)

    def third(b):
        @pl.loop(0, here)
        def _(source):
            back_to_sibling(b, source, 1 - core).wait_recv()
            back_products(source, b * 2 + 1 - core)

    def done(b):
        @pl.when(jnp.logical_and(b <= chip, chip < chips - 1))
        def _():
            to_right(b).wait_send()

        @pl.when(jnp.logical_and(b >= chip, chip > 0))
        def _():
            to_left(b).wait_send()

        to_sibling(b, core).wait_send()

        @pl.loop(here + 1, sections)
        def _(section):
            to_section(b, here, section).wait_send()

        @pl.loop(0, here)
        def _(source):
            back_to_sibling(b, source, core).wait_send()

    @pl.loop(0, 2 * (chips + 2))
    def _(turn_no):
        side = turn_no % 2
        for lag, act in enumerate((arrived, second, third)):
            away = turn_no // 2 - lag
            b = jnp.where(side == 1, chip + away, chip - away)
            first = jnp.where(side == 1, 1, 0)
            fits = jnp.logical_and(b >= 0, b < chips)
            pl.when(jnp.logical_and(fits, away >= first))(functools.partial(act, b))

    def att_to(source, section):
        return remote(
            att, att_in.at[source], att_send.at[section], att_recv.at[source], section, member
        )

    def term_to(source, target):
        return remote(
            c_out.at[target],
            c_in.at[source - 1],
            c_send.at[target],
            c_recv.at[source - 1],
            target,
            member,
        )

    inv = lax.rsqrt(squares[...] / x_ref.shape[1] + 1e-05)
    cos_full, sin_full, keep = cos_ref[...], sin_ref[...], keep_ref[...]
    scale = head ** (-0.5)
    proj[:, : 3 * head] = proj[:, : 3 * head] * inv
    query = turn(proj[:, :head], cos_full, sin_full).astype(BF16)
    keys = turn(proj[:, head : 2 * head], cos_full, sin_full).astype(BF16)
    values = proj[:, 2 * head : 3 * head].astype(BF16)
    scores = dot_cols(query, keys) * scale * keep + (keep - 1.0) * 1e30
    expd = jnp.exp(scores - jnp.max(scores, axis=1, keepdims=True)) * keep
    probs = expd / jnp.sum(expd, axis=1, keepdims=True)
    probs_b = probs.astype(BF16)
    att[...] = dot(probs_b, values).astype(BF16)

    @pl.loop(here + 1, sections)
    def _(section):
        att_to(here, section).start()

    @pl.loop(here + 1, sections)
    def _(source):
        term_to(source, here).wait_recv()
        proj[:, 3 * head :] += c_in[source - 1].astype(F32)

    grad_att = proj[:, 3 * head :].astype(BF16)
    grad_probs = dot_cols(grad_att, values)
    grad_scores = (
        probs * (grad_probs - jnp.sum(grad_probs * probs, axis=1, keepdims=True)) * scale
    ).astype(BF16)
    grad_proj = jnp.concatenate(
        [
            turn(dot(grad_scores, keys), cos_full, -sin_full),
            turn(dot_rows(grad_scores, query), cos_full, -sin_full),
            dot_rows(probs_b, grad_att),
        ],
        axis=1,
    ).astype(BF16)
    grad_wide = grad_proj.astype(F32)
    shift = jnp.sum(grad_wide * proj[:, : 3 * head], axis=1, keepdims=True) / x_ref.shape[1]
    own_rhs[...] = (grad_wide * inv).astype(BF16)
    part = inv * inv * shift

    @pl.loop(0, here)
    def _(step):
        target = here - 1 - step
        term = inv * dot(grad_proj, cross[target].astype(BF16)) - part * through[target]
        c_out[target] = term.astype(BF16)
        term_to(here, target).start()

    low_rhs[...] = jnp.zeros_like(low_rhs)
    mixed[...] = jnp.zeros_like(mixed)

    @pl.loop(0, here)
    def _(source):
        att_to(source, here).wait_recv()
        low = att_in[source]
        low_rhs[source] = (low.astype(F32) * part).astype(BF16)
        mixed[source] = dot_rows(own_rhs[...], low).astype(BF16)

    pl.loop(0, chips)(done)

    @pl.loop(here + 1, sections)
    def _(section):
        att_to(here, section).wait_send()

    @pl.loop(0, here)
    def _(target):
        term_to(here, target).wait_send()


def gathered(sections, members, w_rows, x, up, cos_full, sin_full, keep):
    rows, cols = w_rows.shape
    head = cols // 4
    tokens = x.shape[0]
    chips = members // 2
    lower = sections - 1
    vmem = pl.BlockSpec(memory_space=pltpu.VMEM)
    dma = pltpu.SemaphoreType.DMA
    return pl.pallas_call(
        functools.partial(gather_kernel, sections, chips),
        out_shape=(
            jax.ShapeDtypeStruct((members, rows, cols), BF16),
            jax.ShapeDtypeStruct((tokens, 3 * head), BF16),
            jax.ShapeDtypeStruct((lower, tokens, head), BF16),
            jax.ShapeDtypeStruct((lower, 3 * head, head), BF16),
            jax.ShapeDtypeStruct((tokens, head), BF16),
        ),
        in_specs=[vmem] * 6,
        out_specs=(vmem,) * 5,
        scratch_shapes=[
            pltpu.VMEM((tokens, cols), F32),
            pltpu.VMEM((tokens, 1), F32),
            pltpu.VMEM((lower, tokens, head), F32),
            pltpu.VMEM((lower, 3 * head, head), F32),
            pltpu.VMEM((lower, members, rows, head), BF16),
            pltpu.VMEM((lower, tokens, head), BF16),
            pltpu.VMEM((lower, tokens, head), BF16),
            pltpu.VMEM((lower, tokens, head), BF16),
            dma((chips,)),
            dma((chips,)),
            dma((chips,)),
            dma((chips,)),
            dma((chips,)),
            dma((lower, chips)),
            dma((sections, chips)),
            dma((lower, chips)),
            dma((lower, chips)),
            dma((sections,)),
            dma((lower,)),
            dma((lower,)),
            dma((lower,)),
        ],
        compiler_params=pltpu.CompilerParams(
            collective_id=0, has_side_effects=True, vmem_limit_bytes=VMEM_BYTES
        ),
        cost_estimate=pl.CostEstimate(
            flops=2 * tokens * members * rows * cols, bytes_accessed=1 << 23, transcendentals=0
        ),
    )(w_rows, x, up, cos_full, sin_full, keep)


def scatter_kernel(
    sections,
    chips,
    x_ref,
    up_ref,
    full,
    own_rhs,
    low_rhs,
    mixed,
    att,
    w_ref,
    gain_ref,
    out,
    gains,
    acc,
    sib_out,
    sib_in,
    sibx_out,
    sibx_in,
    x_in,
    z_out,
    z_in,
    sib_send,
    sib_recv,
    sibx_send,
    sibx_recv,
    x_send,
    x_recv,
    z_send,
    z_recv,
    g_send,
    g_recv,
):
    here = lax.axis_index("section")
    member = lax.axis_index("fsdp")
    members = 2 * chips
    chip = member // 2
    core = member % 2
    sibling = chip * 2 + 1 - core
    rows = w_ref.shape[0]
    head = w_ref.shape[1] // 4
    wide = pl.ds(0, 3 * head)
    last = pl.ds(3 * head, head)

    barrier = pltpu.get_barrier_semaphore()

    @pl.loop(1, sections)
    def _(step):
        pl.semaphore_signal(
            barrier,
            inc=1,
            device_id=(lax.rem(here + step, sections), member),
            device_id_type=MESH,
        )

    @pl.loop(1, members)
    def _(step):
        pl.semaphore_signal(
            barrier, inc=1, device_id=(here, lax.rem(member + step, members)), device_id_type=MESH
        )

    pl.semaphore_wait(barrier, sections - 1 + members - 1)

    def columns(idx):
        return pl.ds(pl.multiple_of(idx * rows, rows), rows)

    def to_sibling(b):
        return remote(sib_out.at[b], sib_in.at[b], sib_send.at[b], sib_recv.at[b], here, sibling)

    def low_to_sibling(b, target):
        return remote(
            sibx_out.at[target, b],
            sibx_in.at[target, b],
            sibx_send.at[target, b],
            sibx_recv.at[target, b],
            here,
            sibling,
        )

    def to_section(b, source, target):
        return remote(
            sibx_in.at[target, b],
            x_in.at[source - 1, b],
            x_send.at[target, b],
            x_recv.at[source - 1, b],
            target,
            member,
        )

    def hop(b, part, side):
        cols = last if part else wide
        return remote(
            z_out.at[b, :, cols],
            z_in.at[side, b, :, cols],
            z_send.at[part, b],
            z_recv.at[part, side, b],
            here,
            member - 2 if side else member + 2,
        )

    def gain_to(other):
        return remote(
            gains.at[member], gains.at[member], g_send.at[other], g_recv.at[member], here, other
        )

    def gain_from(other):
        return remote(
            gains.at[other], gains.at[other], g_send.at[other], g_recv.at[other], here, other
        )

    def for_lower(idx, target):
        return dot(full[idx, :, wide], mixed[target]) - dot_rows(
            x_ref[:, columns(idx)], low_rhs[target]
        )

    def far_first(act):
        @pl.loop(0, 2 * chips)
        def _(turn_no):
            side = turn_no % 2
            away = turn_no // 2
            b = jnp.where(side == 1, away, chips - 1 - away)
            fits = jnp.where(side == 1, jnp.where(b < chip, 1, 0), jnp.where(b > chip, 1, 0))

            @pl.when(fits == 1)
            def _():
                act(b)

        act(chip)

    def for_sibling(b):
        idx = b * 2 + 1 - core

        @pl.loop(0, here)
        def _(target):
            sibx_out[target, b] = for_lower(idx, target).astype(BF16)
            low_to_sibling(b, target).start()

        sib_out[b, :, wide] = dot_rows(x_ref[:, columns(idx)], own_rhs[...]).astype(BF16)
        sib_out[b, :, last] = dot_rows(up_ref[:, columns(idx)], att[...]).astype(BF16)
        to_sibling(b).start()

    def for_sections(b):
        @pl.loop(0, here)
        def _(target):
            mine = for_lower(b * 2 + core, target)
            low_to_sibling(b, target).wait_recv()
            both = mine + sibx_in[target, b].astype(F32)
            sibx_in[target, b] = both.astype(BF16)
            to_section(b, here, target).start()

    def along(b, part):
        cols = last if part else wide

        @pl.when(jnp.logical_and(b >= chip, chip > 0))
        def _():
            hop(b, part, 0).wait_recv()
            acc[:, cols] += z_in[0, b, :, cols].astype(F32)

        @pl.when(jnp.logical_and(b <= chip, chip < chips - 1))
        def _():
            hop(b, part, 1).wait_recv()
            acc[:, cols] += z_in[1, b, :, cols].astype(F32)

        @pl.when(b != chip)
        def _():
            z_out[b, :, cols] = acc[:, cols].astype(BF16)

        @pl.when(b > chip)
        def _():
            hop(b, part, 0).start()

        @pl.when(b < chip)
        def _():
            hop(b, part, 1).start()

    def first_part(b):
        mine = dot_rows(x_ref[:, columns(b * 2 + core)], own_rhs[...])
        to_sibling(b).wait_recv()
        acc[:, wide] = mine + sib_in[b, :, wide].astype(F32)
        along(b, 0)

    def second_part(b):
        acc[:, last] = dot_rows(up_ref[:, columns(b * 2 + core)], att[...]) + sib_in[
            b, :, last
        ].astype(F32)

        @pl.loop(here + 1, sections)
        def _(source):
            to_section(b, source, here).wait_recv()
            acc[:, last] += x_in[source - 1, b].astype(F32)

        along(b, 1)

    far_first(for_sibling)
    far_first(for_sections)
    far_first(first_part)

    raw = acc[:, wide]
    out[:, wide] = raw * gain_ref[...]
    gain_rows = jnp.sum(raw * w_ref[:, wide].astype(F32), axis=1, keepdims=True)
    gains[member] = jnp.transpose(jnp.broadcast_to(gain_rows, (rows, 128)))[:8]

    @pl.loop(1, members)
    def _(step):
        gain_to(lax.rem(member + step, members)).start()

    far_first(second_part)
    out[:, last] = acc[:, last]

    @pl.loop(0, chips)
    def _(b):
        to_sibling(b).wait_send()

        @pl.loop(0, here)
        def _(target):
            low_to_sibling(b, target).wait_send()
            to_section(b, here, target).wait_send()

        @pl.when(b != chip)
        def _():
            hop(b, 0, 0).wait_send()
            hop(b, 1, 0).wait_send()

    @pl.loop(1, members)
    def _(step):
        other = lax.rem(member + step, members)
        gain_from(other).wait_recv()
        gain_to(other).wait_send()


def scattered(sections, members, x, up, full, own_rhs, low_rhs, mixed, att, w_own, gain_col):
    rows, cols = w_own.shape
    head = cols // 4
    chips = members // 2
    lower = sections - 1
    vmem = pl.BlockSpec(memory_space=pltpu.VMEM)
    dma = pltpu.SemaphoreType.DMA
    return pl.pallas_call(
        functools.partial(scatter_kernel, sections, chips),
        out_shape=(
            jax.ShapeDtypeStruct((rows, cols), F32),
            jax.ShapeDtypeStruct((members, 8, rows), F32),
        ),
        in_specs=[vmem] * 9,
        out_specs=(vmem,) * 2,
        scratch_shapes=[
            pltpu.VMEM((rows, cols), F32),
            pltpu.VMEM((chips, rows, cols), BF16),
            pltpu.VMEM((chips, rows, cols), BF16),
            pltpu.VMEM((lower, chips, rows, head), BF16),
            pltpu.VMEM((lower, chips, rows, head), BF16),
            pltpu.VMEM((lower, chips, rows, head), BF16),
            pltpu.VMEM((chips, rows, cols), BF16),
            pltpu.VMEM((2, chips, rows, cols), BF16),
            dma((chips,)),
            dma((chips,)),
            dma((lower, chips)),
            dma((lower, chips)),
            dma((lower, chips)),
            dma((lower, chips)),
            dma((2, chips)),
            dma((2, 2, chips)),
            dma((members,)),
            dma((members,)),
        ],
        compiler_params=pltpu.CompilerParams(
            collective_id=1, has_side_effects=True, vmem_limit_bytes=VMEM_BYTES
        ),
        cost_estimate=pl.CostEstimate(
            flops=2 * x.size * cols, bytes_accessed=1 << 23, transcendentals=0
        ),
    )(x, up, full, own_rhs, low_rhs, mixed, att, w_own, gain_col)


def on_device(inputs, upstream, weights, gain):
    sections = lax.axis_size("section")
    micro_count, length, width = inputs.shape[1:]
    head = weights.shape[2] // 4
    tokens = micro_count * length
    x = inputs[0].reshape(tokens, width)
    up = upstream.reshape(tokens, width)
    w_own = weights[0].astype(F32)
    gain_own = gain[0].astype(F32)[:, None]
    w_scaled = (w_own[:, : 3 * head] * gain_own).astype(BF16)
    w_back_own = weights[0][:, 3 * head :]

    members = lax.axis_size("fsdp")
    cosine, sine = rope_tables(length, head)
    cos_full = jnp.tile(jnp.concatenate([cosine, cosine], axis=1), (micro_count, 1))
    sin_full = jnp.tile(jnp.concatenate([-sine, sine], axis=1), (micro_count, 1))
    row = lax.broadcasted_iota(jnp.int32, (tokens, tokens), 0)
    col = lax.broadcasted_iota(jnp.int32, (tokens, tokens), 1)
    keep = jnp.logical_and(row // length == col // length, row >= col).astype(F32)
    full, own_rhs, low_rhs, mixed, att = gathered(
        sections,
        members,
        jnp.concatenate([w_scaled, w_back_own], axis=1),
        x,
        up,
        cos_full,
        sin_full,
        keep,
    )
    shard, gains = scattered(
        sections,
        members,
        x,
        up,
        full,
        own_rhs,
        low_rhs,
        mixed,
        att,
        weights[0],
        gain_own,
    )
    return (shard[None], gains[:, 0, :].reshape(1, width))


def solution(mesh):
    return jax.shard_map(
        on_device,
        mesh=mesh,
        in_specs=(
            P("section", None, "fsdp", None),
            P(None, "fsdp", None),
            P("section", "fsdp", None),
            P("section", "fsdp"),
        ),
        out_specs=(P("section", "fsdp", None), P("section", None)),
        check_vma=False,
    )
```

```python
import functools

import jax
import jax.numpy as jnp
import numpy as np
from jax import lax
from jax.experimental import pallas as pl
from jax.experimental.pallas import tpu as pltpu
from jax.sharding import PartitionSpec as P

MESH = pl.DeviceIdType.MESH
VMEM_BYTES = 56 * 1024 * 1024

F32 = jnp.float32
BF16 = jnp.bfloat16


def tables(micro_count, length, head):
    freq = 500000.0 ** (-2.0 * np.arange(head // 2) / head)
    angle = np.arange(length)[:, None] * freq[None, :]
    cosine, sine = np.cos(angle), np.sin(angle)
    cos_full = np.tile(np.concatenate([cosine, cosine], axis=1), (micro_count, 1))
    sin_full = np.tile(np.concatenate([-sine, sine], axis=1), (micro_count, 1))
    token = np.arange(micro_count * length)
    same = token[:, None] // length == token[None, :] // length
    keep = np.logical_and(same, token[:, None] >= token[None, :])
    return tuple(jnp.asarray(table.astype(np.float32)) for table in (cos_full, sin_full, keep))


def turn(rows, cos_full, sin_full):
    return rows * cos_full + pltpu.roll(rows, rows.shape[-1] // 2, 1) * sin_full


def dot(left, right):
    return jnp.dot(left, right, preferred_element_type=F32)


def dot_rows(left, right):
    return lax.dot_general(left, right, (((0,), (0,)), ((), ())), preferred_element_type=F32)


def dot_cols(left, right):
    return lax.dot_general(left, right, (((1,), (1,)), ((), ())), preferred_element_type=F32)


def remote(src, dst, send_sem, recv_sem, section, member):
    return pltpu.make_async_remote_copy(
        src_ref=src,
        dst_ref=dst,
        send_sem=send_sem,
        recv_sem=recv_sem,
        device_id=(section, member),
        device_id_type=MESH,
    )


def layer_kernel(
    sections,
    chips,
    w_ref,
    gain_ref,
    x_ref,
    up_ref,
    cos_ref,
    sin_ref,
    keep_ref,
    out,
    gain_out,
    full,
    gain_col,
    own_rhs,
    low_rhs,
    mixed,
    att,
    proj,
    squares,
    through,
    cross,
    back,
    att_in,
    c_out,
    c_in,
    acc,
    sib_out,
    sib_in,
    x_in,
    z_out,
    z_in,
    gains,
    ready,
    z_recv,
    z_right,
    z_left,
    sib_recv,
    sib_send,
    x_recv,
    x_send,
    sibx_recv,
    sibx_send,
    att_send,
    att_recv,
    c_send,
    c_recv,
    sum_send,
    sum_recv,
    low_send,
    low_recv,
    e_send,
    e_recv,
    zs_send,
    zs_recv,
    g_send,
    g_recv,
):
    here = lax.axis_index("section")
    member = lax.axis_index("fsdp")
    members = 2 * chips
    chip = member // 2
    core = member % 2
    sibling = chip * 2 + 1 - core
    rows = w_ref.shape[0]
    head = w_ref.shape[1] // 4
    wide = pl.ds(0, 3 * head)
    last = pl.ds(3 * head, head)
    gain_col[...] = jnp.transpose(jnp.broadcast_to(gain_ref[...].astype(F32), (128, rows)))
    full[member, :, wide] = (w_ref[:, wide].astype(F32) * gain_col[:, :1]).astype(BF16)
    full[member, :, last] = w_ref[:, last]
    proj[...] = jnp.zeros_like(proj)
    squares[...] = jnp.zeros_like(squares)
    through[...] = jnp.zeros_like(through)
    cross[...] = jnp.zeros_like(cross)

    barrier = pltpu.get_barrier_semaphore()

    @pl.loop(1, sections)
    def _(step):
        pl.semaphore_signal(
            barrier,
            inc=1,
            device_id=(lax.rem(here + step, sections), member),
            device_id_type=MESH,
        )

    @pl.loop(1, members)
    def _(step):
        pl.semaphore_signal(
            barrier, inc=1, device_id=(here, lax.rem(member + step, members)), device_id_type=MESH
        )

    pl.semaphore_wait(barrier, sections - 1 + members - 1)

    def to_right(b):
        block = full.at[b * 2 + core]
        return remote(block, block, z_right.at[b], z_recv.at[b], here, member + 2)

    def to_left(b):
        block = full.at[b * 2 + core]
        return remote(block, block, z_left.at[b], z_recv.at[b], here, member - 2)

    def to_sibling(b, lane):
        block = full.at[b * 2 + lane]
        return remote(block, block, sib_send.at[b], sib_recv.at[b], here, sibling)

    def to_section(b, source, section):
        return remote(
            full.at[b * 2 + core, :, pl.ds(3 * head, head)],
            back.at[source, b * 2 + core],
            x_send.at[section, b],
            x_recv.at[source, b],
            section,
            member,
        )

    def back_to_sibling(b, source, lane):
        block = back.at[source, b * 2 + lane]
        return remote(
            block, block, sibx_send.at[source, b], sibx_recv.at[source, b], here, sibling
        )

    def columns(idx):
        return pl.ds(pl.multiple_of(idx * rows, rows), rows)

    def products(idx):
        part_x = x_ref[:, columns(idx)].astype(F32)
        squares[...] += jnp.sum(part_x * part_x, axis=1, keepdims=True)
        proj[:, : 3 * head] += dot(x_ref[:, columns(idx)], full[idx, :, : 3 * head])
        proj[:, 3 * head :] += dot(up_ref[:, columns(idx)], full[idx, :, 3 * head :])

    def back_products(source, idx):
        through[source] += dot(x_ref[:, columns(idx)], back[source, idx])
        cross[source] += dot_rows(full[idx, :, : 3 * head], back[source, idx])

    def arrived(b):
        @pl.when(b < chip)
        def _():
            to_right(b).wait_recv()

        @pl.when(b > chip)
        def _():
            to_left(b).wait_recv()

        @pl.when(jnp.logical_and(b <= chip, chip < chips - 1))
        def _():
            to_right(b).start()

        @pl.when(jnp.logical_and(b >= chip, chip > 0))
        def _():
            to_left(b).start()

        to_sibling(b, core).start()

        @pl.loop(here + 1, sections)
        def _(section):
            to_section(b, here, section).start()

        products(b * 2 + core)

    def second(b):
        to_sibling(b, 1 - core).wait_recv()
        products(b * 2 + 1 - core)

        @pl.loop(0, here)
        def _(source):
            to_section(b, source, here).wait_recv()
            back_to_sibling(b, source, core).start()
            back_products(source, b * 2 + core)

    def third(b):
        @pl.loop(0, here)
        def _(source):
            back_to_sibling(b, source, 1 - core).wait_recv()
            back_products(source, b * 2 + 1 - core)

    def done(b):
        @pl.when(jnp.logical_and(b <= chip, chip < chips - 1))
        def _():
            to_right(b).wait_send()

        @pl.when(jnp.logical_and(b >= chip, chip > 0))
        def _():
            to_left(b).wait_send()

        to_sibling(b, core).wait_send()

        @pl.loop(here + 1, sections)
        def _(section):
            to_section(b, here, section).wait_send()

        @pl.loop(0, here)
        def _(source):
            back_to_sibling(b, source, core).wait_send()

    @pl.loop(0, 2 * (chips + 2))
    def _(turn_no):
        side = turn_no % 2
        for lag, act in enumerate((arrived, second, third)):
            away = turn_no // 2 - lag
            b = jnp.where(side == 1, chip + away, chip - away)
            first = jnp.where(side == 1, 1, 0)
            fits = jnp.logical_and(b >= 0, b < chips)
            pl.when(jnp.logical_and(fits, away >= first))(functools.partial(act, b))

    def att_to(source, section):
        return remote(
            att, att_in.at[source], att_send.at[section], att_recv.at[source], section, member
        )

    def term_to(source, target):
        return remote(
            c_out.at[target],
            c_in.at[source - 1],
            c_send.at[target],
            c_recv.at[source - 1],
            target,
            member,
        )

    inv = lax.rsqrt(squares[...] / x_ref.shape[1] + 1e-05)
    cos_full, sin_full, keep = cos_ref[...], sin_ref[...], keep_ref[...]
    scale = head ** (-0.5)
    proj[:, : 3 * head] = proj[:, : 3 * head] * inv
    query = turn(proj[:, :head], cos_full, sin_full).astype(BF16)
    keys = turn(proj[:, head : 2 * head], cos_full, sin_full).astype(BF16)
    values = proj[:, 2 * head : 3 * head].astype(BF16)
    scores = dot_cols(query, keys) * scale * keep + (keep - 1.0) * 1e30
    expd = jnp.exp(scores - jnp.max(scores, axis=1, keepdims=True)) * keep
    probs = expd / jnp.sum(expd, axis=1, keepdims=True)
    probs_b = probs.astype(BF16)
    att[...] = dot(probs_b, values).astype(BF16)

    @pl.loop(here + 1, sections)
    def _(section):
        att_to(here, section).start()

    @pl.loop(here + 1, sections)
    def _(source):
        term_to(source, here).wait_recv()
        proj[:, 3 * head :] += c_in[source - 1].astype(F32)

    grad_att = proj[:, 3 * head :].astype(BF16)
    grad_probs = dot_cols(grad_att, values)
    grad_scores = (
        probs * (grad_probs - jnp.sum(grad_probs * probs, axis=1, keepdims=True)) * scale
    ).astype(BF16)
    grad_proj = jnp.concatenate(
        [
            turn(dot(grad_scores, keys), cos_full, -sin_full),
            turn(dot_rows(grad_scores, query), cos_full, -sin_full),
            dot_rows(probs_b, grad_att),
        ],
        axis=1,
    ).astype(BF16)
    grad_wide = grad_proj.astype(F32)
    shift = jnp.sum(grad_wide * proj[:, : 3 * head], axis=1, keepdims=True) / x_ref.shape[1]
    own_rhs[...] = (grad_wide * inv).astype(BF16)
    part = inv * inv * shift

    @pl.loop(0, here)
    def _(step):
        target = here - 1 - step
        term = inv * dot(grad_proj, cross[target].astype(BF16)) - part * through[target]
        c_out[target] = term.astype(BF16)
        term_to(here, target).start()

    low_rhs[...] = jnp.zeros_like(low_rhs)
    mixed[...] = jnp.zeros_like(mixed)

    @pl.loop(0, here)
    def _(source):
        att_to(source, here).wait_recv()
        low = att_in[source]
        low_rhs[source] = (low.astype(F32) * part).astype(BF16)
        mixed[source] = dot_rows(own_rhs[...], low).astype(BF16)

    pl.loop(0, chips)(done)

    @pl.loop(here + 1, sections)
    def _(section):
        att_to(here, section).wait_send()

    @pl.loop(0, here)
    def _(target):
        term_to(here, target).wait_send()

    def sum_to_sibling(b):
        return remote(sib_out.at[b], sib_in.at[b], sum_send.at[b], sum_recv.at[b], here, sibling)

    def low_to_sibling(b, target):
        return remote(
            back.at[target, 2 * b],
            back.at[target, 2 * b + 1],
            low_send.at[target, b],
            low_recv.at[target, b],
            here,
            sibling,
        )

    def low_to_section(b, source, target):
        return remote(
            back.at[target, 2 * b + 1],
            x_in.at[source - 1, b],
            e_send.at[target, b],
            e_recv.at[source - 1, b],
            target,
            member,
        )

    def hop(b, part, side):
        cols = last if part else wide
        return remote(
            z_out.at[b, :, cols],
            z_in.at[side, b, :, cols],
            zs_send.at[part, b],
            zs_recv.at[part, side, b],
            here,
            member - 2 if side else member + 2,
        )

    def gain_to(other):
        return remote(
            gains.at[:, columns(member)], gains.at[:, columns(member)], g_send.at[other], g_recv.at[member], here, other
        )

    def gain_from(other):
        return remote(
            gains.at[:, columns(other)], gains.at[:, columns(other)], g_send.at[other], g_recv.at[other], here, other
        )

    def for_lower(idx, target):
        return dot(full[idx, :, wide], mixed[target]) - dot_rows(
            x_ref[:, columns(idx)], low_rhs[target]
        )

    def far_first(act):
        @pl.loop(0, 2 * chips)
        def _(turn_no):
            side = turn_no % 2
            away = turn_no // 2
            b = jnp.where(side == 1, away, chips - 1 - away)
            fits = jnp.where(side == 1, jnp.where(b < chip, 1, 0), jnp.where(b > chip, 1, 0))

            @pl.when(fits == 1)
            def _():
                act(b)

        act(chip)

    def low_for_sibling(b):
        @pl.loop(0, here)
        def _(target):
            back[target, 2 * b] = for_lower(b * 2 + 1 - core, target).astype(BF16)
            low_to_sibling(b, target).start()

    def for_sibling(b):
        idx = b * 2 + 1 - core
        sib_out[b, :, wide] = dot_rows(x_ref[:, columns(idx)], own_rhs[...]).astype(BF16)
        sib_out[b, :, last] = dot_rows(up_ref[:, columns(idx)], att[...]).astype(BF16)
        sum_to_sibling(b).start()

    def for_sections(b):
        @pl.loop(0, here)
        def _(target):
            mine = for_lower(b * 2 + core, target)
            low_to_sibling(b, target).wait_recv()
            both = mine + back[target, 2 * b + 1].astype(F32)
            back[target, 2 * b + 1] = both.astype(BF16)
            low_to_section(b, here, target).start()

    def along(b, part):
        cols = last if part else wide

        @pl.when(jnp.logical_and(b >= chip, chip > 0))
        def _():
            hop(b, part, 0).wait_recv()
            acc[:, cols] += z_in[0, b, :, cols].astype(F32)

        @pl.when(jnp.logical_and(b <= chip, chip < chips - 1))
        def _():
            hop(b, part, 1).wait_recv()
            acc[:, cols] += z_in[1, b, :, cols].astype(F32)

        @pl.when(b != chip)
        def _():
            z_out[b, :, cols] = acc[:, cols].astype(BF16)

        @pl.when(b > chip)
        def _():
            hop(b, part, 0).start()

        @pl.when(b < chip)
        def _():
            hop(b, part, 1).start()

    def first_part(b):
        mine = dot_rows(x_ref[:, columns(b * 2 + core)], own_rhs[...])
        sum_to_sibling(b).wait_recv()
        acc[:, wide] = mine + sib_in[b, :, wide].astype(F32)
        along(b, 0)

    def second_part(b):
        acc[:, last] = dot_rows(up_ref[:, columns(b * 2 + core)], att[...]) + sib_in[
            b, :, last
        ].astype(F32)

        @pl.loop(here + 1, sections)
        def _(source):
            low_to_section(b, source, here).wait_recv()
            acc[:, last] += x_in[source - 1, b].astype(F32)

        along(b, 1)

    pl.semaphore_signal(ready, inc=1, device_id=(here, sibling), device_id_type=MESH)
    far_first(for_sibling)
    pl.semaphore_wait(ready, 1)
    far_first(low_for_sibling)
    far_first(for_sections)
    far_first(first_part)

    raw = acc[:, wide]
    out[:, wide] = raw * gain_col[:, :1]
    gain_rows = jnp.sum(raw * w_ref[:, wide].astype(F32), axis=1, keepdims=True)
    gains[:, columns(member)] = jnp.transpose(jnp.broadcast_to(gain_rows, (rows, 128)))[:8]

    @pl.loop(1, members)
    def _(step):
        gain_to(lax.rem(member + step, members)).start()

    far_first(second_part)
    out[:, last] = acc[:, last]

    @pl.loop(0, chips)
    def _(b):
        sum_to_sibling(b).wait_send()

        @pl.loop(0, here)
        def _(target):
            low_to_sibling(b, target).wait_send()
            low_to_section(b, here, target).wait_send()

        @pl.when(b != chip)
        def _():
            hop(b, 0, 0).wait_send()
            hop(b, 1, 0).wait_send()

    @pl.loop(1, members)
    def _(step):
        other = lax.rem(member + step, members)
        gain_from(other).wait_recv()
        gain_to(other).wait_send()
    gain_out[...] = gains[:1]


def layer(sections, members, w_own, gain_row, x, up, cos_full, sin_full, keep):
    rows, cols = w_own.shape
    head = cols // 4
    tokens = x.shape[0]
    chips = members // 2
    lower = sections - 1
    vmem = pl.BlockSpec(memory_space=pltpu.VMEM)
    dma = pltpu.SemaphoreType.DMA
    return pl.pallas_call(
        functools.partial(layer_kernel, sections, chips),
        out_shape=(
            jax.ShapeDtypeStruct((rows, cols), F32),
            jax.ShapeDtypeStruct((1, members * rows), F32),
        ),
        in_specs=[vmem] * 7,
        out_specs=(vmem,) * 2,
        scratch_shapes=[
            pltpu.VMEM((members, rows, cols), BF16),
            pltpu.VMEM((rows, 128), F32),
            pltpu.VMEM((tokens, 3 * head), BF16),
            pltpu.VMEM((lower, tokens, head), BF16),
            pltpu.VMEM((lower, 3 * head, head), BF16),
            pltpu.VMEM((tokens, head), BF16),
            pltpu.VMEM((tokens, cols), F32),
            pltpu.VMEM((tokens, 1), F32),
            pltpu.VMEM((lower, tokens, head), F32),
            pltpu.VMEM((lower, 3 * head, head), F32),
            pltpu.VMEM((lower, members, rows, head), BF16),
            pltpu.VMEM((lower, tokens, head), BF16),
            pltpu.VMEM((lower, tokens, head), BF16),
            pltpu.VMEM((lower, tokens, head), BF16),
            pltpu.VMEM((rows, cols), F32),
            pltpu.VMEM((chips, rows, cols), BF16),
            pltpu.VMEM((chips, rows, cols), BF16),
            pltpu.VMEM((lower, chips, rows, head), BF16),
            pltpu.VMEM((chips, rows, cols), BF16),
            pltpu.VMEM((2, chips, rows, cols), BF16),
            pltpu.VMEM((8, members * rows), F32),
            pltpu.SemaphoreType.REGULAR,
            dma((chips,)),
            dma((chips,)),
            dma((chips,)),
            dma((chips,)),
            dma((chips,)),
            dma((lower, chips)),
            dma((sections, chips)),
            dma((lower, chips)),
            dma((lower, chips)),
            dma((sections,)),
            dma((lower,)),
            dma((lower,)),
            dma((lower,)),
            dma((chips,)),
            dma((chips,)),
            dma((lower, chips)),
            dma((lower, chips)),
            dma((lower, chips)),
            dma((lower, chips)),
            dma((2, chips)),
            dma((2, 2, chips)),
            dma((members,)),
            dma((members,)),
        ],
        compiler_params=pltpu.CompilerParams(
            collective_id=0, has_side_effects=True, vmem_limit_bytes=VMEM_BYTES
        ),
        cost_estimate=pl.CostEstimate(
            flops=6 * x.size * cols, bytes_accessed=1 << 23, transcendentals=0
        ),
    )(w_own, gain_row, x, up, cos_full, sin_full, keep)


def on_device(inputs, upstream, weights, gain):
    micro_count, length, width = inputs.shape[1:]
    head = weights.shape[2] // 4
    tokens = micro_count * length
    cos_full, sin_full, keep = tables(micro_count, length, head)
    shard, gain_sum = layer(
        lax.axis_size("section"),
        lax.axis_size("fsdp"),
        weights[0],
        gain,
        inputs[0].reshape(tokens, width),
        upstream.reshape(tokens, width),
        cos_full,
        sin_full,
        keep,
    )
    return (shard[None], gain_sum)


def solution(mesh):
    return jax.shard_map(
        on_device,
        mesh=mesh,
        in_specs=(
            P("section", None, "fsdp", None),
            P(None, "fsdp", None),
            P("section", "fsdp", None),
            P("section", "fsdp"),
        ),
        out_specs=(P("section", "fsdp", None), P("section", None)),
        check_vma=False,
    )
```

```python
import functools

import jax
import jax.numpy as jnp
import numpy as np
from jax import lax
from jax.experimental import pallas as pl
from jax.experimental.pallas import tpu as pltpu
from jax.sharding import PartitionSpec as P

MESH = pl.DeviceIdType.MESH
VMEM_BYTES = 62 * 1024 * 1024

F32 = jnp.float32
BF16 = jnp.bfloat16


def tables(micro_count, length, head):
    freq = 500000.0 ** (-2.0 * np.arange(head // 2) / head)
    angle = np.arange(length)[:, None] * freq[None, :]
    cosine, sine = np.cos(angle), np.sin(angle)
    cos_full = np.tile(np.concatenate([cosine, cosine], axis=1), (micro_count, 1))
    sin_full = np.tile(np.concatenate([-sine, sine], axis=1), (micro_count, 1))
    token = np.arange(micro_count * length)
    same = token[:, None] // length == token[None, :] // length
    keep = np.logical_and(same, token[:, None] >= token[None, :])
    return tuple(jnp.asarray(table.astype(np.float32)) for table in (cos_full, sin_full, keep))


def turn(rows, cos_full, sin_full):
    return rows * cos_full + pltpu.roll(rows, rows.shape[-1] // 2, 1) * sin_full


def dot(left, right):
    return jnp.dot(left, right, preferred_element_type=F32)


def dot_rows(left, right):
    return lax.dot_general(left, right, (((0,), (0,)), ((), ())), preferred_element_type=F32)


def dot_cols(left, right):
    return lax.dot_general(left, right, (((1,), (1,)), ((), ())), preferred_element_type=F32)


def remote(src, dst, send_sem, recv_sem, section, member):
    return pltpu.make_async_remote_copy(
        src_ref=src,
        dst_ref=dst,
        send_sem=send_sem,
        recv_sem=recv_sem,
        device_id=(section, member),
        device_id_type=MESH,
    )


def layer_kernel(
    sections,
    chips,
    w_ref,
    gain_ref,
    x_ref,
    up_ref,
    cos_ref,
    sin_ref,
    keep_ref,
    out,
    gain_out,
    full,
    gain_col,
    x_turned,
    up_turned,
    w_turned,
    own_rhs,
    low_rhs,
    mixed,
    att,
    proj,
    squares,
    through,
    cross,
    back,
    att_in,
    c_out,
    c_in,
    acc,
    sib_out,
    sib_in,
    x_in,
    z_out,
    z_in,
    gains,
    ready,
    z_recv,
    z_right,
    z_left,
    sib_recv,
    sib_send,
    x_recv,
    x_send,
    sibx_recv,
    sibx_send,
    att_send,
    att_recv,
    c_send,
    c_recv,
    sum_send,
    sum_recv,
    low_send,
    low_recv,
    e_send,
    e_recv,
    zs_send,
    zs_recv,
    g_send,
    g_recv,
):
    here = lax.axis_index("section")
    member = lax.axis_index("fsdp")
    members = 2 * chips
    chip = member // 2
    core = member % 2
    sibling = chip * 2 + 1 - core
    rows = w_ref.shape[0]
    head = w_ref.shape[1] // 4
    wide = pl.ds(0, 3 * head)
    last = pl.ds(3 * head, head)
    gain_col[...] = jnp.transpose(jnp.broadcast_to(gain_ref[...].astype(F32), (128, rows)))
    full[member, :, wide] = (w_ref[:, wide].astype(F32) * gain_col[:, :1]).astype(BF16)
    full[member, :, last] = w_ref[:, last]
    proj[...] = jnp.zeros_like(proj)
    squares[...] = jnp.zeros_like(squares)
    through[...] = jnp.zeros_like(through)
    cross[...] = jnp.zeros_like(cross)

    barrier = pltpu.get_barrier_semaphore()

    @pl.loop(1, sections)
    def _(step):
        pl.semaphore_signal(
            barrier,
            inc=1,
            device_id=(lax.rem(here + step, sections), member),
            device_id_type=MESH,
        )

    @pl.loop(1, members)
    def _(step):
        pl.semaphore_signal(
            barrier, inc=1, device_id=(here, lax.rem(member + step, members)), device_id_type=MESH
        )

    pl.semaphore_wait(barrier, sections - 1 + members - 1)

    def to_right(b):
        block = full.at[b * 2 + core]
        return remote(block, block, z_right.at[b], z_recv.at[b], here, member + 2)

    def to_left(b):
        block = full.at[b * 2 + core]
        return remote(block, block, z_left.at[b], z_recv.at[b], here, member - 2)

    def to_sibling(b, lane):
        block = full.at[b * 2 + lane]
        return remote(block, block, sib_send.at[b], sib_recv.at[b], here, sibling)

    def to_section(b, source, section):
        return remote(
            full.at[b * 2 + core, :, pl.ds(3 * head, head)],
            back.at[source, b * 2 + core],
            x_send.at[section, b],
            x_recv.at[source, b],
            section,
            member,
        )

    def back_to_sibling(b, source, lane):
        block = back.at[source, b * 2 + lane]
        return remote(
            block, block, sibx_send.at[source, b], sibx_recv.at[source, b], here, sibling
        )

    def columns(idx):
        return pl.ds(pl.multiple_of(idx * rows, rows), rows)

    def products(idx):
        x_turned[idx] = jnp.transpose(x_ref[:, columns(idx)])
        up_turned[idx] = jnp.transpose(up_ref[:, columns(idx)])
        w_turned[idx] = jnp.transpose(full[idx, :, : 3 * head])
        part_x = x_ref[:, columns(idx)].astype(F32)
        squares[...] += jnp.sum(part_x * part_x, axis=1, keepdims=True)
        proj[:, : 3 * head] += dot(x_ref[:, columns(idx)], full[idx, :, : 3 * head])
        proj[:, 3 * head :] += dot(up_ref[:, columns(idx)], full[idx, :, 3 * head :])

    def back_products(source, idx):
        through[source] += dot(x_ref[:, columns(idx)], back[source, idx])
        cross[source] += dot(w_turned[idx], back[source, idx])

    def arrived(b):
        @pl.when(b < chip)
        def _():
            to_right(b).wait_recv()

        @pl.when(b > chip)
        def _():
            to_left(b).wait_recv()

        @pl.when(jnp.logical_and(b <= chip, chip < chips - 1))
        def _():
            to_right(b).start()

        @pl.when(jnp.logical_and(b >= chip, chip > 0))
        def _():
            to_left(b).start()

        to_sibling(b, core).start()

        @pl.loop(here + 1, sections)
        def _(section):
            to_section(b, here, section).start()

        products(b * 2 + core)

    def second(b):
        to_sibling(b, 1 - core).wait_recv()
        products(b * 2 + 1 - core)

        @pl.loop(0, here)
        def _(source):
            to_section(b, source, here).wait_recv()
            back_to_sibling(b, source, core).start()
            back_products(source, b * 2 + core)

    def third(b):
        @pl.loop(0, here)
        def _(source):
            back_to_sibling(b, source, 1 - core).wait_recv()
            back_products(source, b * 2 + 1 - core)

    def done(b):
        @pl.when(jnp.logical_and(b <= chip, chip < chips - 1))
        def _():
            to_right(b).wait_send()

        @pl.when(jnp.logical_and(b >= chip, chip > 0))
        def _():
            to_left(b).wait_send()

        to_sibling(b, core).wait_send()

        @pl.loop(here + 1, sections)
        def _(section):
            to_section(b, here, section).wait_send()

        @pl.loop(0, here)
        def _(source):
            back_to_sibling(b, source, core).wait_send()

    @pl.loop(0, 2 * (chips + 2))
    def _(turn_no):
        side = turn_no % 2
        for lag, act in enumerate((arrived, second, third)):
            away = turn_no // 2 - lag
            b = jnp.where(side == 1, chip + away, chip - away)
            first = jnp.where(side == 1, 1, 0)
            fits = jnp.logical_and(b >= 0, b < chips)
            pl.when(jnp.logical_and(fits, away >= first))(functools.partial(act, b))

    def att_to(source, section):
        return remote(
            att, att_in.at[source], att_send.at[section], att_recv.at[source], section, member
        )

    def term_to(source, target):
        return remote(
            c_out.at[target],
            c_in.at[source - 1],
            c_send.at[target],
            c_recv.at[source - 1],
            target,
            member,
        )

    inv = lax.rsqrt(squares[...] / x_ref.shape[1] + 1e-05)
    cos_full, sin_full, keep = cos_ref[...], sin_ref[...], keep_ref[...]
    scale = head ** (-0.5)
    proj[:, : 3 * head] = proj[:, : 3 * head] * inv
    query = turn(proj[:, :head], cos_full, sin_full).astype(BF16)
    keys = turn(proj[:, head : 2 * head], cos_full, sin_full).astype(BF16)
    values = proj[:, 2 * head : 3 * head].astype(BF16)
    scores = dot_cols(query, keys) * scale * keep + (keep - 1.0) * 1e30
    expd = jnp.exp(scores - jnp.max(scores, axis=1, keepdims=True)) * keep
    probs = expd / jnp.sum(expd, axis=1, keepdims=True)
    probs_b = probs.astype(BF16)
    att[...] = dot(probs_b, values).astype(BF16)

    @pl.loop(here + 1, sections)
    def _(section):
        att_to(here, section).start()

    @pl.loop(here + 1, sections)
    def _(source):
        term_to(source, here).wait_recv()
        proj[:, 3 * head :] += c_in[source - 1].astype(F32)

    grad_att = proj[:, 3 * head :].astype(BF16)
    grad_probs = dot_cols(grad_att, values)
    grad_scores = (
        probs * (grad_probs - jnp.sum(grad_probs * probs, axis=1, keepdims=True)) * scale
    ).astype(BF16)
    grad_proj = jnp.concatenate(
        [
            turn(dot(grad_scores, keys), cos_full, -sin_full),
            turn(dot_rows(grad_scores, query), cos_full, -sin_full),
            dot_rows(probs_b, grad_att),
        ],
        axis=1,
    ).astype(BF16)
    grad_wide = grad_proj.astype(F32)
    shift = jnp.sum(grad_wide * proj[:, : 3 * head], axis=1, keepdims=True) / x_ref.shape[1]
    own_rhs[...] = (grad_wide * inv).astype(BF16)
    part = inv * inv * shift

    @pl.loop(0, here)
    def _(step):
        target = here - 1 - step
        term = inv * dot(grad_proj, cross[target].astype(BF16)) - part * through[target]
        c_out[target] = term.astype(BF16)
        term_to(here, target).start()

    low_rhs[...] = jnp.zeros_like(low_rhs)
    mixed[...] = jnp.zeros_like(mixed)

    @pl.loop(0, here)
    def _(source):
        att_to(source, here).wait_recv()
        low = att_in[source]
        low_rhs[source] = (low.astype(F32) * part).astype(BF16)
        mixed[source] = dot_rows(own_rhs[...], low).astype(BF16)

    pl.loop(0, chips)(done)

    @pl.loop(here + 1, sections)
    def _(section):
        att_to(here, section).wait_send()

    @pl.loop(0, here)
    def _(target):
        term_to(here, target).wait_send()

    def sum_to_sibling(b):
        return remote(sib_out.at[b], sib_in.at[b], sum_send.at[b], sum_recv.at[b], here, sibling)

    def low_to_sibling(b, target):
        return remote(
            back.at[target, 2 * b],
            back.at[target, 2 * b + 1],
            low_send.at[target, b],
            low_recv.at[target, b],
            here,
            sibling,
        )

    def low_to_section(b, source, target):
        return remote(
            back.at[target, 2 * b + 1],
            x_in.at[source - 1, b],
            e_send.at[target, b],
            e_recv.at[source - 1, b],
            target,
            member,
        )

    def hop(b, part, side):
        cols = last if part else wide
        return remote(
            z_out.at[b, :, cols],
            z_in.at[side, b, :, cols],
            zs_send.at[part, b],
            zs_recv.at[part, side, b],
            here,
            member - 2 if side else member + 2,
        )

    def gain_to(other):
        return remote(
            gains.at[:, columns(member)], gains.at[:, columns(member)], g_send.at[other], g_recv.at[member], here, other
        )

    def gain_from(other):
        return remote(
            gains.at[:, columns(other)], gains.at[:, columns(other)], g_send.at[other], g_recv.at[other], here, other
        )

    def for_lower(idx, target):
        return dot(full[idx, :, wide], mixed[target]) - dot(x_turned[idx], low_rhs[target])

    def far_first(act):
        @pl.loop(0, 2 * chips)
        def _(turn_no):
            side = turn_no % 2
            away = turn_no // 2
            b = jnp.where(side == 1, away, chips - 1 - away)
            fits = jnp.where(side == 1, jnp.where(b < chip, 1, 0), jnp.where(b > chip, 1, 0))

            @pl.when(fits == 1)
            def _():
                act(b)

        act(chip)

    def low_for_sibling(b):
        @pl.loop(0, here)
        def _(target):
            back[target, 2 * b] = for_lower(b * 2 + 1 - core, target).astype(BF16)
            low_to_sibling(b, target).start()

    def for_sibling(b):
        idx = b * 2 + 1 - core
        sib_out[b, :, wide] = dot(x_turned[idx], own_rhs[...]).astype(BF16)
        sib_out[b, :, last] = dot(up_turned[idx], att[...]).astype(BF16)
        sum_to_sibling(b).start()

    def for_sections(b):
        @pl.loop(0, here)
        def _(target):
            mine = for_lower(b * 2 + core, target)
            low_to_sibling(b, target).wait_recv()
            both = mine + back[target, 2 * b + 1].astype(F32)
            back[target, 2 * b + 1] = both.astype(BF16)
            low_to_section(b, here, target).start()

    def along(b, part):
        cols = last if part else wide

        @pl.when(jnp.logical_and(b >= chip, chip > 0))
        def _():
            hop(b, part, 0).wait_recv()
            acc[:, cols] += z_in[0, b, :, cols].astype(F32)

        @pl.when(jnp.logical_and(b <= chip, chip < chips - 1))
        def _():
            hop(b, part, 1).wait_recv()
            acc[:, cols] += z_in[1, b, :, cols].astype(F32)

        @pl.when(b != chip)
        def _():
            z_out[b, :, cols] = acc[:, cols].astype(BF16)

        @pl.when(b > chip)
        def _():
            hop(b, part, 0).start()

        @pl.when(b < chip)
        def _():
            hop(b, part, 1).start()

    def first_part(b):
        mine = dot(x_turned[b * 2 + core], own_rhs[...])
        sum_to_sibling(b).wait_recv()
        acc[:, wide] = mine + sib_in[b, :, wide].astype(F32)
        along(b, 0)

    def second_part(b):
        acc[:, last] = dot(up_turned[b * 2 + core], att[...]) + sib_in[
            b, :, last
        ].astype(F32)

        @pl.loop(here + 1, sections)
        def _(source):
            low_to_section(b, source, here).wait_recv()
            acc[:, last] += x_in[source - 1, b].astype(F32)

        along(b, 1)

    pl.semaphore_signal(ready, inc=1, device_id=(here, sibling), device_id_type=MESH)
    far_first(for_sibling)
    pl.semaphore_wait(ready, 1)
    far_first(low_for_sibling)
    far_first(for_sections)
    far_first(first_part)

    raw = acc[:, wide]
    out[:, wide] = raw * gain_col[:, :1]
    gain_rows = jnp.sum(raw * w_ref[:, wide].astype(F32), axis=1, keepdims=True)
    gains[:, columns(member)] = jnp.transpose(jnp.broadcast_to(gain_rows, (rows, 128)))[:8]

    @pl.loop(1, members)
    def _(step):
        gain_to(lax.rem(member + step, members)).start()

    far_first(second_part)
    out[:, last] = acc[:, last]

    @pl.loop(0, chips)
    def _(b):
        sum_to_sibling(b).wait_send()

        @pl.loop(0, here)
        def _(target):
            low_to_sibling(b, target).wait_send()
            low_to_section(b, here, target).wait_send()

        @pl.when(b != chip)
        def _():
            hop(b, 0, 0).wait_send()
            hop(b, 1, 0).wait_send()

    @pl.loop(1, members)
    def _(step):
        other = lax.rem(member + step, members)
        gain_from(other).wait_recv()
        gain_to(other).wait_send()
    gain_out[...] = gains[:1]


def layer(sections, members, w_own, gain_row, x, up, cos_full, sin_full, keep):
    rows, cols = w_own.shape
    head = cols // 4
    tokens = x.shape[0]
    chips = members // 2
    lower = sections - 1
    vmem = pl.BlockSpec(memory_space=pltpu.VMEM)
    dma = pltpu.SemaphoreType.DMA
    return pl.pallas_call(
        functools.partial(layer_kernel, sections, chips),
        out_shape=(
            jax.ShapeDtypeStruct((rows, cols), F32),
            jax.ShapeDtypeStruct((1, members * rows), F32),
        ),
        in_specs=[vmem] * 7,
        out_specs=(vmem,) * 2,
        scratch_shapes=[
            pltpu.VMEM((members, rows, cols), BF16),
            pltpu.VMEM((rows, 128), F32),
            pltpu.VMEM((members, rows, tokens), BF16),
            pltpu.VMEM((members, rows, tokens), BF16),
            pltpu.VMEM((members, 3 * head, rows), BF16),
            pltpu.VMEM((tokens, 3 * head), BF16),
            pltpu.VMEM((lower, tokens, head), BF16),
            pltpu.VMEM((lower, 3 * head, head), BF16),
            pltpu.VMEM((tokens, head), BF16),
            pltpu.VMEM((tokens, cols), F32),
            pltpu.VMEM((tokens, 1), F32),
            pltpu.VMEM((lower, tokens, head), F32),
            pltpu.VMEM((lower, 3 * head, head), F32),
            pltpu.VMEM((lower, members, rows, head), BF16),
            pltpu.VMEM((lower, tokens, head), BF16),
            pltpu.VMEM((lower, tokens, head), BF16),
            pltpu.VMEM((lower, tokens, head), BF16),
            pltpu.VMEM((rows, cols), F32),
            pltpu.VMEM((chips, rows, cols), BF16),
            pltpu.VMEM((chips, rows, cols), BF16),
            pltpu.VMEM((lower, chips, rows, head), BF16),
            pltpu.VMEM((chips, rows, cols), BF16),
            pltpu.VMEM((2, chips, rows, cols), BF16),
            pltpu.VMEM((8, members * rows), F32),
            pltpu.SemaphoreType.REGULAR,
            dma((chips,)),
            dma((chips,)),
            dma((chips,)),
            dma((chips,)),
            dma((chips,)),
            dma((lower, chips)),
            dma((sections, chips)),
            dma((lower, chips)),
            dma((lower, chips)),
            dma((sections,)),
            dma((lower,)),
            dma((lower,)),
            dma((lower,)),
            dma((chips,)),
            dma((chips,)),
            dma((lower, chips)),
            dma((lower, chips)),
            dma((lower, chips)),
            dma((lower, chips)),
            dma((2, chips)),
            dma((2, 2, chips)),
            dma((members,)),
            dma((members,)),
        ],
        compiler_params=pltpu.CompilerParams(
            collective_id=0, has_side_effects=True, vmem_limit_bytes=VMEM_BYTES
        ),
        cost_estimate=pl.CostEstimate(
            flops=6 * x.size * cols, bytes_accessed=1 << 23, transcendentals=0
        ),
    )(w_own, gain_row, x, up, cos_full, sin_full, keep)


def on_device(inputs, upstream, weights, gain):
    micro_count, length, width = inputs.shape[1:]
    head = weights.shape[2] // 4
    tokens = micro_count * length
    cos_full, sin_full, keep = tables(micro_count, length, head)
    shard, gain_sum = layer(
        lax.axis_size("section"),
        lax.axis_size("fsdp"),
        weights[0],
        gain,
        inputs[0].reshape(tokens, width),
        upstream.reshape(tokens, width),
        cos_full,
        sin_full,
        keep,
    )
    return (shard[None], gain_sum)


def solution(mesh):
    return jax.shard_map(
        on_device,
        mesh=mesh,
        in_specs=(
            P("section", None, "fsdp", None),
            P(None, "fsdp", None),
            P("section", "fsdp", None),
            P("section", "fsdp"),
        ),
        out_specs=(P("section", "fsdp", None), P("section", None)),
        check_vma=False,
    )
```
